512 devices in a mesh: gx: 32 (over x_hi, z), gy: 16 (over y, x_lo, core).
Axes of the slice: x: 4 (x_hi: 2, x_lo: 2; x = x_hi * 2 + x_lo), y: 4, z: 16, core: 2. Of those that a mesh axis runs over, the one named last changes fastest.
Arguments:
- flow_pops: float32 [19, 192, 128, 128], P(None, 'gx', 'gy'), may hold values from 0 to 0.5, as said below
- warmth_distribution: float32 [7, 192, 128, 128], P(None, 'gx', 'gy'), may hold values from 0 to 0.65, as said below
- fill_mass: float32 [192, 128, 128], P('gx', 'gy'), may hold values from 0.1 to 1
- diffusivity: float32 [192, 128, 128], P('gx', 'gy'), may hold values from 0.02 to 0.3
- heat_source: float32 [192, 128, 128], P('gx', 'gy'), may hold values from 0 to 0.2
- cell_kind: int32 [192, 128, 128], P('gx', 'gy'), may hold values from 0 to 3, as said below
- fill_masks: int32 [2, 192, 128, 128], P(None, 'gx', 'gy'), may hold values from 0 to 511
Outputs:
- flow_out: float32 [19, 192, 128, 128], P(None, 'gx', 'gy')
- heat_out: float32 [7, 192, 128, 128], P(None, 'gx', 'gy')
- mass_out: float32 [192, 128, 128], P('gx', 'gy')
The draws below stay inside these ranges and needn't reach their ends.
Inputs may be any that keep to these rules, and one draw needn't show every extreme that they name: `cell_kind`: outermost cells in x and y and the bottom layer in z are walls; each column holds liquid below gas, with its surface at any height; a non-wall non-gas cell is interface exactly when one of its 18 neighbours is gas. `flow_pops`: each population is its lattice weight times a factor in 0.5 to 1.5. `warmth_distribution`: each population is its lattice weight times a positive temperature-like factor.
All inputs are finite; a program needn't handle non-finite values.
Results may differ from the reference program's by a relative error of at most 0.0003.
Values sent between devices are 32-bit elements; how exact they have to be, the bound alone decides.
A program may use at most 64 MiB of HBM per device.

```python
import math
import jax
import jax.numpy as jnp
import numpy as np
from jax import lax

CX = 6
NZ = 128
ITERS = 3
NX = 192
NY = 128


def draw_flow_pops(key, part):
    key = jax.random.fold_in(key, 11)
    weights = jnp.array([1.0 / 3.0] + [1.0 / 18.0] * 6 + [1.0 / 36.0] * 12, dtype=jnp.float32)
    noise = jax.random.uniform(key, (19, NX, NY, NZ), jnp.float32, -1.0, 1.0)
    return (weights[:, None, None, None] * (1.0 + 0.5 * noise)).astype(jnp.float32)


def draw_warmth_distribution(key, part):
    key = jax.random.fold_in(key, 23)
    first_key, second_key = jax.random.split(key)
    weights = jnp.array([0.25] + [0.125] * 6, dtype=jnp.float32)
    base = jax.random.uniform(first_key, (NX, NY, NZ), jnp.float32, 0.0, 1.0)
    level = 0.5 + 1.5 * base
    noise = jax.random.uniform(second_key, (7, NX, NY, NZ), jnp.float32, -1.0, 1.0)
    return (weights[:, None, None, None] * level[None] * (1.0 + 0.3 * noise)).astype(jnp.float32)


def draw_cell_kind(key, part):
    key = jax.random.fold_in(key, 37)
    level_key, noise_key = jax.random.split(key)
    band_count = NX // CX
    centers = jax.random.randint(level_key, (band_count,), 6, NZ - 5, dtype=jnp.int32)
    noise = jax.random.randint(noise_key, (NX, NY), -12, 13, dtype=jnp.int32)
    band_index = jnp.arange(NX, dtype=jnp.int32) // CX
    amplitude = 1 + 6 * (band_index % 4)
    height = centers[band_index][:, None] + noise * amplitude[:, None] // 12
    height = jnp.clip(height, 1, NZ - 2)
    depth = jnp.arange(NZ, dtype=jnp.int32)
    xs = jnp.arange(NX, dtype=jnp.int32)[:, None, None]
    ys = jnp.arange(NY, dtype=jnp.int32)[None, :, None]
    walls = (xs == 0) | (xs == NX - 1) | (ys == 0) | (ys == NY - 1) | (depth[None, None, :] == 0)
    gaseous = (depth[None, None, :] > height[:, :, None]) & jnp.logical_not(walls)
    nearby = jnp.zeros_like(gaseous)
    offsets = [(1, 0, 0), (-1, 0, 0), (0, 1, 0), (0, -1, 0), (0, 0, 1), (0, 0, -1), (1, 1, 0), (-1, -1, 0), (1, -1, 0), (-1, 1, 0), (1, 0, 1), (-1, 0, -1), (1, 0, -1), (-1, 0, 1), (0, 1, 1), (0, -1, -1), (0, 1, -1), (0, -1, 1)]
    for offset in offsets:
        nearby = nearby | jnp.roll(gaseous, offset, (0, 1, 2))
    kinds = jnp.where(walls, 3, jnp.where(gaseous, 0, jnp.where(nearby, 1, 2)))
    return kinds.astype(jnp.int32)


def set_ends(entries, own_key, least, top_value):
    extent = entries.shape
    spot = [jax.random.randint(jax.random.fold_in(own_key, axis), (), 0, extent[axis]) for axis in range(len(extent))]
    entries = entries.at[tuple(spot)].set(least)
    longest = extent.index(max(extent))
    spot[longest] = (spot[longest] + 1) % extent[longest]
    return entries.at[tuple(spot)].set(top_value)


def steps_of(own_key, shape, pieces, smallest, largest):
    level = 1.0
    for position, shards_of in pieces:
        steps = jax.random.uniform(jax.random.fold_in(jax.random.fold_in(own_key, 6), position), (shards_of,), jnp.float32, smallest / len(pieces), largest / len(pieces))
        level = level * jnp.repeat(jnp.exp(steps), shape[position] // shards_of).reshape((-1,) + (1,) * (len(shape) - 1 - position))
    return level


def setup_inputs(seed: int = 0) -> dict:
    key_of = jax.random.split(jax.random.key(seed), 8)
    return {
        "flow_pops": draw_flow_pops(jax.random.fold_in(key_of[7], 71), 0),
        "warmth_distribution": draw_warmth_distribution(jax.random.fold_in(key_of[7], 71), 0),
        "fill_mass": jnp.clip(0.1 + 0.9 * jax.random.uniform(key_of[2], (NX, NY, NZ), jnp.float32) ** steps_of(key_of[2], (NX, NY, NZ), ((0, 32), (1, 16)), -0.2, 0.2), 0.1, 1.0),
        "diffusivity": jnp.clip(jnp.exp(math.log(0.3) - 2.7080503 * jax.random.uniform(key_of[3], (NX, NY, NZ), jnp.float32) ** steps_of(key_of[3], (NX, NY, NZ), ((0, 32), (1, 16)), -0.2, 0.2)), 0.02, 0.3),
        "heat_source": jnp.clip(0.2 * jax.random.uniform(key_of[4], (NX, NY, NZ), jnp.float32) ** steps_of(key_of[4], (NX, NY, NZ), ((0, 32), (1, 16)), -0.2, 0.2), 0.0, 0.2),
        "cell_kind": draw_cell_kind(jax.random.fold_in(key_of[7], 71), 0),
        "fill_masks": set_ends(jax.random.randint(key_of[6], (2, NX, NY, NZ), 0, 512), jax.random.fold_in(key_of[6], 1), 0, 511).astype(jnp.int32),
    }


VELOCITY = [(0, 0, 0), (1, 0, 0), (-1, 0, 0), (0, 1, 0), (0, -1, 0), (0, 0, 1), (0, 0, -1),
            (1, 1, 0), (-1, -1, 0), (1, -1, 0), (-1, 1, 0), (1, 0, 1), (-1, 0, -1), (1, 0, -1),
            (-1, 0, 1), (0, 1, 1), (0, -1, -1), (0, 1, -1), (0, -1, 1)]
WEIGHTS = [1.0 / 3.0] + [1.0 / 18.0] * 6 + [1.0 / 36.0] * 12
OPPOSITE = [0, 2, 1, 4, 3, 6, 5, 8, 7, 10, 9, 12, 11, 14, 13, 16, 15, 18, 17]
WARMTH_LATTICE_W = [0.25] + [0.125] * 6
expansion_factor = 0.05


def relaxation_matrix():
    table = np.array(VELOCITY)
    px, py, pz = table[:, 0], table[:, 1], table[:, 2]
    sq = px * px + py * py + pz * pz
    rows = [px * 0 + 1.0, 19 * sq - 30.0, (21 * sq * sq - 53 * sq + 24) / 2.0, px * 1.0, (5 * sq - 9) * px * 1.0,
            py * 1.0, (5 * sq - 9) * py * 1.0, pz * 1.0, (5 * sq - 9) * pz * 1.0, 3 * px * px - sq * 1.0,
            (3 * sq - 5) * (3 * px * px - sq) * 1.0, py * py - pz * pz * 1.0, (3 * sq - 5) * (py * py - pz * pz) * 1.0,
            px * py * 1.0, py * pz * 1.0, px * pz * 1.0, (py * py - pz * pz) * px * 1.0, (pz * pz - px * px) * py * 1.0,
            (px * px - py * py) * pz * 1.0]
    moment = np.stack(rows)
    inverse = moment.T / np.sum(moment * moment, axis=1)
    rates = np.array([0.0, 1.19, 1.4, 0.0, 1.2, 0.0, 1.2, 0.0, 1.2, 1.25, 1.4, 1.25, 1.4, 1.25, 1.25, 1.25, 1.98, 1.98, 1.98])
    return (inverse * rates[None, :]) @ moment


def flow_moments(flow_pops):
    density = jnp.sum(flow_pops, axis=0)
    momenta = []
    for axis_pick in range(3):
        total = jnp.zeros_like(density)
        for i in range(19):
            if VELOCITY[i][axis_pick] == 1:
                total = total + flow_pops[i]
            elif VELOCITY[i][axis_pick] == -1:
                total = total - flow_pops[i]
        momenta.append(total / density)
    return density, momenta[0], momenta[1], momenta[2]


def equilibrium(i, density, vel_x, vel_y, vel_z, speed_sq):
    dir_x, dir_y, dir_z = VELOCITY[i]
    projected_speed = dir_x * vel_x + dir_y * vel_y + dir_z * vel_z
    return WEIGHTS[i] * density * (1.0 + 3.0 * projected_speed + 4.5 * projected_speed * projected_speed - 1.5 * speed_sq)


def collision(flow_pops, warmth_distribution, fill_mass, diffusivity, heat_source, cell_kind):
    density, vel_x, vel_y, vel_z = flow_moments(flow_pops)
    speed_sq = vel_x * vel_x + vel_y * vel_y + vel_z * vel_z
    cellwise_warmth = jnp.sum(warmth_distribution, axis=0)
    balance = jnp.stack([equilibrium(i, density, vel_x, vel_y, vel_z, speed_sq) for i in range(19)])
    kernel = jnp.asarray(relaxation_matrix(), dtype=jnp.float32)
    relaxed = jnp.einsum("ij,jxyz->ixyz", kernel, flow_pops - balance, precision=lax.Precision.HIGHEST)
    lifting_push = expansion_factor * (cellwise_warmth - 1.0)
    post_flow = jnp.stack([flow_pops[i] - relaxed[i] + (3.0 * WEIGHTS[i] * VELOCITY[i][2]) * lifting_push
                           for i in range(19)])
    relax_rate = 1.0 / (0.5 + 4.0 * diffusivity)
    post_list = []
    for warmth_lattice_vector in range(7):
        dir_x, dir_y, dir_z = VELOCITY[warmth_lattice_vector]
        projected_speed = dir_x * vel_x + dir_y * vel_y + dir_z * vel_z
        warmth_rest_state = WARMTH_LATTICE_W[warmth_lattice_vector] * cellwise_warmth * (1.0 + 4.0 * projected_speed)
        post_list.append(warmth_distribution[warmth_lattice_vector] - relax_rate * (warmth_distribution[warmth_lattice_vector] - warmth_rest_state) + WARMTH_LATTICE_W[warmth_lattice_vector] * heat_source)
    post_heat = jnp.stack(post_list)
    fill_frac = jnp.where(cell_kind == 1, fill_mass / density, jnp.where(cell_kind == 2, 1.0, 0.0))
    return post_flow, post_heat, fill_frac


def shift_depth(values, dir_z):
    if dir_z == 1:
        return jnp.concatenate([jnp.zeros_like(values[..., :1]), values[..., :-1]], axis=-1)
    if dir_z == -1:
        return jnp.concatenate([values[..., 1:], jnp.zeros_like(values[..., :1])], axis=-1)
    return values


def pull_from(padded, i, rows, cols):
    dir_x, dir_y, dir_z = VELOCITY[i]
    return shift_depth(padded[1 - dir_x:1 - dir_x + rows, 1 - dir_y:1 - dir_y + cols], dir_z)


def running(populations, frac_pad, kind_pad, flow_pops, warmth_distribution, fill_mass, fill_masks, cell_kind):
    rows, cols = flow_pops.shape[1], flow_pops.shape[2]
    post_flow = populations[:19, 1:-1, 1:-1]
    post_heat = populations[19:, 1:-1, 1:-1]
    fill_frac = frac_pad[1:-1, 1:-1]
    density, vel_x, vel_y, vel_z = flow_moments(flow_pops)
    speed_sq = vel_x * vel_x + vel_y * vel_y + vel_z * vel_z
    unit_rho = jnp.ones_like(density)
    read = [post_flow[0]]
    mass_change = jnp.zeros_like(density)
    for i in range(1, 19):
        source_kind = pull_from(kind_pad, i, rows, cols)
        incoming = pull_from(populations[i], i, rows, cols)
        bounced = post_flow[OPPOSITE[i]]
        rebuilt = (equilibrium(i, unit_rho, vel_x, vel_y, vel_z, speed_sq)
                   + equilibrium(OPPOSITE[i], unit_rho, vel_x, vel_y, vel_z, speed_sq) - bounced)
        read.append(jnp.where(source_kind == 3, bounced, jnp.where(source_kind == 0, rebuilt, incoming)))
        exchange_weight = jnp.where(source_kind == 2, 1.0,
                                    jnp.where(source_kind == 1, 0.5 * (fill_frac + pull_from(frac_pad, i, rows, cols)), 0.0))
        mask_word = fill_masks[(i - 1) // 9]
        enabled = ((mask_word // (2 ** ((i - 1) % 9))) % 2).astype(density.dtype)
        mass_change = mass_change + enabled * exchange_weight * (incoming - bounced)
    heat_read = [post_heat[0]]
    for warmth_lattice_vector in range(1, 7):
        source_kind = pull_from(kind_pad, warmth_lattice_vector, rows, cols)
        incoming = pull_from(populations[19 + warmth_lattice_vector], warmth_lattice_vector, rows, cols)
        bounced = post_heat[OPPOSITE[warmth_lattice_vector]]
        heat_read.append(jnp.where((source_kind == 0) | (source_kind == 3), bounced, incoming))
    fluid = (cell_kind == 1) | (cell_kind == 2)
    flow_next = jnp.where(fluid[None], jnp.stack(read), flow_pops)
    heat_next = jnp.where(fluid[None], jnp.stack(heat_read), warmth_distribution)
    new_density = jnp.sum(flow_next, axis=0)
    mass_next = jnp.where(cell_kind == 1, fill_mass + mass_change, jnp.where(cell_kind == 2, new_density, 0.0))
    return flow_next, heat_next, mass_next


def reference(flow_pops, warmth_distribution, fill_mass, diffusivity, heat_source, cell_kind, fill_masks):
    plane = ((1, 1), (1, 1), (0, 0))
    for iteration in range(ITERS):
        flow_pad = jnp.pad(flow_pops, ((0, 0),) + plane)
        heat_pad = jnp.pad(warmth_distribution, ((0, 0),) + plane)
        mass_pad = jnp.pad(fill_mass, plane)
        diff_pad = jnp.pad(diffusivity, plane)
        source_pad = jnp.pad(heat_source, plane)
        kind_pad = jnp.pad(cell_kind, plane)

        def one_block(block_index):
            first_row = block_index * CX
            flow_slab = lax.dynamic_slice_in_dim(flow_pad, first_row, CX + 2, 1)
            heat_slab = lax.dynamic_slice_in_dim(heat_pad, first_row, CX + 2, 1)
            mass_slab = lax.dynamic_slice_in_dim(mass_pad, first_row, CX + 2, 0)
            diff_slab = lax.dynamic_slice_in_dim(diff_pad, first_row, CX + 2, 0)
            source_slab = lax.dynamic_slice_in_dim(source_pad, first_row, CX + 2, 0)
            kind_slab = lax.dynamic_slice_in_dim(kind_pad, first_row, CX + 2, 0)
            post_flow, post_heat, fill_frac = collision(flow_slab, heat_slab, mass_slab, diff_slab, source_slab, kind_slab)
            populations = jnp.concatenate([post_flow, post_heat], axis=0)
            mask_slab = lax.dynamic_slice_in_dim(fill_masks, first_row, CX, 1)
            return running(populations, fill_frac, kind_slab, flow_slab[:, 1:-1, 1:-1],
                             heat_slab[:, 1:-1, 1:-1], mass_slab[1:-1, 1:-1], mask_slab, kind_slab[1:-1, 1:-1])

        flow_blocks, heat_blocks, mass_blocks = lax.map(one_block, jnp.arange(NX // CX, dtype=jnp.int32))
        flow_pops = jnp.moveaxis(flow_blocks, 0, 1).reshape(19, NX, NY, NZ)
        warmth_distribution = jnp.moveaxis(heat_blocks, 0, 1).reshape(7, NX, NY, NZ)
        fill_mass = mass_blocks.reshape(NX, NY, NZ)
    return flow_pops, warmth_distribution, fill_mass
```

```python
import functools

import jax
import jax.numpy as jnp
from jax import lax
from jax.experimental import pallas as pl
from jax.experimental.pallas import tpu as pltpu
from jax.sharding import PartitionSpec as P

ITERS = 3
VELOCITY = [
    (0, 0, 0),
    (1, 0, 0),
    (-1, 0, 0),
    (0, 1, 0),
    (0, -1, 0),
    (0, 0, 1),
    (0, 0, -1),
    (1, 1, 0),
    (-1, -1, 0),
    (1, -1, 0),
    (-1, 1, 0),
    (1, 0, 1),
    (-1, 0, -1),
    (1, 0, -1),
    (-1, 0, 1),
    (0, 1, 1),
    (0, -1, -1),
    (0, 1, -1),
    (0, -1, 1),
]
WEIGHTS = [1.0 / 3.0] + [1.0 / 18.0] * 6 + [1.0 / 36.0] * 12
OPPOSITE = [0, 2, 1, 4, 3, 6, 5, 8, 7, 10, 9, 12, 11, 14, 13, 16, 15, 18, 17]
EXPANSION = 0.05
MESH = pl.DeviceIdType.MESH
ROWS, SUB, LANE = 6, 8, 128

FRAC, KIND_A, KIND_B = 26, 27, 28
X_FIELDS = [
    [KIND_A, 1, 7, 9, 11, 13, 20, FRAC, 2, 8, 10, 12, 14, 21, KIND_B],
    [1, 7, 9, 11, 13, 20, FRAC, 2, 8, 10, 12, 14, 21],
]
Y_FIELDS = [
    {1: [3, 15, 17, 22, KIND_A, 7, FRAC, 10, KIND_B], -1: [4, 16, 18, 23, KIND_A, 9, FRAC, 8, KIND_B]},
    {1: [3, 15, 17, 22, 7, FRAC, 10], -1: [4, 16, 18, 23, 9, FRAC, 8]},
]
CLASSES = [(1, 0), (-1, 0), (1, 1), (1, -1), (-1, 1), (-1, -1), (0, 1), (0, -1)]


def x_index(rd, field):
    return X_FIELDS[min(rd, 1)].index(field)


def y_index(rd, dy, field):
    return Y_FIELDS[min(rd, 1)][dy].index(field)


def roll_y(value, dy):
    return pltpu.roll(value, dy % SUB, 0) if dy else value


def roll_z(value, dz):
    return pltpu.roll(value, dz % LANE, 1) if dz else value


def collide(f, g, mass, rate, heat, kind):
    (sa, sb, sc, sd, se, sf, sg, sh, si) = [f[i] + f[i + 1] for i in range(1, 19, 2)]
    (da, db, dc, dd, de, df, dg, dh, di) = [f[i] - f[i + 1] for i in range(1, 19, 2)]
    sxy, sxz, syz = sd + se, sf + sg, sh + si
    sbc = sb + sc
    sax = sa + sbc
    sdg = sxy + sxz + syz
    rho = f[0] + sax + sdg
    xde, xfg = dd + de, df + dg
    yde, yhi = dd - de, dh + di
    zfg, zhi = df - dg, dh - di
    xs, ys, zs = xde + xfg, yde + yhi, zfg + zhi
    jx, jy, jz = da + xs, db + ys, dc + zs
    inv = 1.0 / rho
    ux, uy, uz = jx * inv, jy * inv, jz * inv
    xx, yy, zz = jx * ux, jy * uy, jz * uz
    ruu = xx + yy + zz
    ae = (1.19 * 19.0 / 2394.0) * (sdg - f[0] - ruu)
    ap = (1.4 / 252.0) * (9.0 * f[0] - 7.0 * sax - 2.0 * sdg + 5.5 * ruu)
    qxx, qww = 2.0 * xx - yy - zz, yy - zz
    t1, t2 = 2.0 * sa - sbc, sxy + sxz - 2.0 * syz
    w1, w2 = sb - sc, sxy - sxz
    b = (1.25 / 36.0) * (t1 + t2 - qxx)
    bp = (1.4 / 72.0) * (t2 - 2.0 * t1 + 0.5 * qxx)
    c = (1.25 / 12.0) * (w1 + w2 - qww)
    cp = (1.4 / 24.0) * (w2 - 2.0 * w1 + 0.5 * qww)
    dxy = (1.25 / 4.0) * (sd - se - jx * uy)
    dyz = (1.25 / 4.0) * (sh - si - jy * uz)
    dxz = (1.25 / 4.0) * (sf - sg - jx * uz)
    q = 1.2 / 40.0 * 5.0 / 3.0
    qx, qy, qz = q * (xs - 2.0 * da), q * (ys - 2.0 * db), q * (zs - 2.0 * dc)
    m = 1.98 / 8.0
    mx, my, mz = m * (xde - xfg), m * (yhi - yde), m * (zfg - zhi)
    b1, b2 = -11.0 * ae - 4.0 * ap, 8.0 * ae + ap
    bm, cm, bs, cs = b - 2.0 * bp, c - 2.0 * cp, b + bp, c + cp
    b1m = b1 - bm
    exy, exz, eyz = b2 + bs + cs, b2 + bs - cs, b2 - 2.0 * bs
    even = [b1m + 3.0 * bm, b1m + cm, b1m - cm, exy + dxy, exy - dxy, exz + dxz, exz - dxz, eyz + dyz, eyz - dyz]
    warmth = g[0] + (g[1] + g[2]) + (g[3] + g[4]) + (g[5] + g[6])
    push = (EXPANSION / 6.0) * (warmth - 1.0)
    half = 0.5 * push
    xp, xm, yp, ym, zp, zm = qx + mx, qx - mx, qy + my, qy - my, qz + mz - half, qz - mz - half
    odd = [-4.0 * qx, -4.0 * qy, -4.0 * qz - push, xp + ym, xp - ym, xm + zp, xm - zp, yp + zm, yp - zm]
    post = [f[0] + 30.0 * ae - 12.0 * ap]
    for k in range(9):
        post.append(f[2 * k + 1] - (even[k] + odd[k]))
        post.append(f[2 * k + 2] - (even[k] - odd[k]))
    keep = 1.0 - rate
    rest = 0.125 * (rate * warmth + heat)
    half_rate = 0.5 * rate * warmth
    post.append(keep * g[0] + 2.0 * rest)
    for k, u in enumerate((ux, uy, uz)):
        move = half_rate * u
        post.append(keep * g[2 * k + 1] + (rest + move))
        post.append(keep * g[2 * k + 2] + (rest - move))
    frac = jnp.where(kind == 1, mass * inv, jnp.where(kind == 2, 1.0, 0.0))
    return post, frac, (ux, uy, uz)


def kernel(gx_size, gy_size, *refs):
    flow_in, heat_in, mass_in, diff_in, source_in, kind_in, mask_in = refs[:7]
    flow_out, heat_out, mass_out = refs[7:10]
    (flow, warm, mass, rate, source, kinds, masks, post, vel, own_frac, t_buf, y_buf, h_buf, code, liquid, shared,
     load_sem, send_sem, recv_sem) = refs[10:]
    gx, gy = lax.axis_index("gx"), lax.axis_index("gy")

    def there(dx, dy):
        tests = []
        if dx:
            tests.append(gx < gx_size - 1 if dx > 0 else gx > 0)
        if dy:
            tests.append(gy < gy_size - 1 if dy > 0 else gy > 0)
        return functools.reduce(jnp.logical_and, tests)

    loads = [
        pltpu.make_async_copy(src, dst, load_sem.at[i])
        for i, (src, dst) in enumerate(
            [(flow_in, flow), (heat_in, warm), (mass_in, mass), (diff_in, rate), (source_in, source), (kind_in, kinds),
             (mask_in, masks)]
        )
    ]
    for load in loads:
        load.start()
    barrier = pltpu.get_barrier_semaphore()
    for dx, dy in CLASSES:

        @pl.when(there(dx, dy))
        def _():
            pl.semaphore_signal(barrier, inc=1, device_id=(gx + dx, gy + dy), device_id_type=MESH)

    def copy_of(rd, cls):
        dx, dy = CLASSES[cls]
        first = rd == 0
        if not dy:
            own, far = (ROWS, 0) if dx > 0 else (1, ROWS + 1)
            if dx > 0:
                fields = pl.ds(0, 8 if first else 7)
            else:
                fields = pl.ds(7 if first else 6, 8 if first else 7)
            src, dst = t_buf.at[rd, fields, own], t_buf.at[rd, fields, far]
        else:
            side, edge = (0, 0) if dy > 0 else (1, SUB - 1)
            line = pl.ds(edge, 1)
            if not dx:
                fields = pl.ds(0, 8 if first else 7)
                own = far = pl.ds(1, ROWS)
            elif dx > 0:
                fields = pl.ds(4, 3 if first else 2)
                own, far = ROWS, 0
            else:
                fields = pl.ds(6 if first else 5, 3 if first else 2)
                own, far = 1, ROWS + 1
            src, dst = y_buf.at[rd, side, fields, own, line], h_buf.at[rd, side, fields, far, line]
        return pltpu.make_async_remote_copy(
            src_ref=src,
            dst_ref=dst,
            send_sem=send_sem.at[rd, cls],
            recv_sem=recv_sem.at[rd, cls],
            device_id=(gx + dx, gy + dy),
            device_id_type=MESH,
        )

    def send(rd, classes):
        for cls in classes:

            @pl.when(there(*CLASSES[cls]))
            def _():
                copy_of(rd, cls).start()

    def receive(rd, classes):
        for cls in classes:
            dx, dy = CLASSES[cls]

            @pl.when(there(-dx, -dy))
            def _():
                copy_of(rd, cls).wait_recv()

    line_of = lax.broadcasted_iota(jnp.int32, (SUB, LANE), 0)
    edge_of = {1: line_of == 0, -1: line_of == SUB - 1}
    top = lax.broadcasted_iota(jnp.int32, (SUB, LANE), 1) == LANE - 1

    def collide_row(rd, r, f, g, m):
        kind = kinds[r]
        if rd == 0:
            rate[r] = 1.0 / (0.5 + 4.0 * rate[r])
        values, frac, velocity = collide(f, g, m, rate[r], source[r], kind)
        for i in range(26):
            post[i, r] = values[i]
        for i in range(3):
            vel[i, r] = velocity[i]
        own_frac[r] = frac
        fields = dict(enumerate(values))
        fields[FRAC] = frac
        if rd == 0:
            fields[KIND_A] = fields[KIND_B] = kind.astype(jnp.float32)
        moved = {}
        for i, field in enumerate(X_FIELDS[min(rd, 1)]):
            value = fields[field]
            if field < 26:
                dx, dy, dz = VELOCITY[field if field < 19 else field - 19]
                value = moved[field] = roll_y(roll_z(value, dz), dy)
            t_buf[rd, i, r + 1] = value
        for side, way in ((0, 1), (1, -1)):
            for i, field in enumerate(Y_FIELDS[min(rd, 1)][way]):
                if field in moved:
                    value = moved[field]
                else:
                    dz = VELOCITY[field if field < 19 else field - 19][2] if field < 26 else 0
                    value = roll_y(roll_z(fields[field], dz), way)
                y_buf[rd, side, i, r + 1] = value

    def joined(rd, way, field, row, value):
        side, edge = (0, 0) if way > 0 else (1, SUB - 1)
        return jnp.where(edge_of[way], h_buf[rd, side, y_index(rd, way, field), row, edge : edge + 1], value)

    def sources(rd, r, field_of, own):
        plain = {0: own, 1: field_of(r), -1: field_of(r + 2)}
        found = {}
        for dx in (0, 1, -1):
            row = r + 1 - dx
            found[dx, 0] = plain[dx]
            for way in (1, -1):
                if isinstance(field_of.name, dict):
                    name = field_of.name[dx]
                else:
                    name = field_of.name
                found[dx, way] = joined(rd, way, name, row, roll_y(plain[dx], way))
        return {i: roll_z(found[VELOCITY[i][0], VELOCITY[i][1]], VELOCITY[i][2]) for i in range(1, 19)}

    def stream_row(rd, r, last_row):
        kind = kinds[r]
        if rd == 0:

            def kind_at(row):
                return t_buf[rd, x_index(rd, KIND_B if last_row and row is not r else KIND_A), row]

            kind_at.name = {0: KIND_A, 1: KIND_A, -1: KIND_B if last_row else KIND_A}
            kind_from = sources(rd, r, kind_at, kind.astype(jnp.float32))

        def frac_at(row):
            return t_buf[rd, x_index(rd, FRAC), row]

        frac_at.name = FRAC
        frac = own_frac[r]
        frac_from = sources(rd, r, frac_at, frac)
        ux, uy, uz = vel[0, r], vel[1, r], vel[2, r]
        base = 2.0 - 3.0 * (ux * ux + uy * uy + uz * uz)
        old = [post[i, r] for i in range(26)]

        def incoming(i):
            dx, dy, dz = VELOCITY[i if i < 19 else i - 19]
            row = r + 1 - dx
            if dx == 0 and dy == 0:
                return roll_z(old[i], dz)
            if dx and not dy:
                return t_buf[rd, x_index(rd, i), row]
            if dx:
                return joined(rd, dy, i, row, t_buf[rd, x_index(rd, i), row])
            return joined(rd, dy, i, row, y_buf[rd, 0 if dy > 0 else 1, y_index(rd, dy, i), row])

        f_new, g_new = [old[0]], [old[19]]
        change = jnp.zeros((SUB, LANE), jnp.float32)
        closed = {}
        for i in range(1, 19):
            if rd == 0:
                word = masks[(i - 1) // 9, r]
                enabled = ((word >> ((i - 1) % 9)) & 1).astype(jnp.float32)
                here = kind_from[i]
                if VELOCITY[i][2] < 0:
                    here = jnp.where(top, 0.0, here)
                code[i - 1, r] = here
                whole = jnp.where(here == 2.0, enabled, 0.0)
                part = jnp.where(here == 1.0, 0.5 * enabled, 0.0)
                liquid[i - 1, r] = whole
                shared[i - 1, r] = part
            else:
                here, whole, part = code[i - 1, r], liquid[i - 1, r], shared[i - 1, r]
            wall, gas = here == 3.0, here == 0.0
            dx, dy, dz = VELOCITY[i]
            along = sum(s * u for s, u in zip((dx, dy, dz), (ux, uy, uz)) if s)
            rebuilt = WEIGHTS[i] * (base + 9.0 * (along * along))
            arriving, back = incoming(i), old[OPPOSITE[i]]
            f_new.append(jnp.where(wall, back, jnp.where(gas, rebuilt - back, arriving)))
            change = change + (whole + part * (frac + frac_from[i])) * (arriving - back)
            if i < 7:
                closed[i] = jnp.logical_or(wall, gas)
        for k in range(1, 7):
            g_new.append(jnp.where(closed[k], old[19 + OPPOSITE[k]], incoming(19 + k)))
        fluid = jnp.logical_or(kind == 1, kind == 2)
        f_new = [jnp.where(fluid, f_new[i], flow[i, r]) for i in range(19)]
        g_new = [jnp.where(fluid, g_new[k], warm[k, r]) for k in range(7)]
        total = functools.reduce(jnp.add, f_new)
        m_new = jnp.where(kind == 1, mass[r] + change, jnp.where(kind == 2, total, 0.0))
        if rd == ITERS - 1:
            for i in range(19):
                flow_out[i, r] = f_new[i]
            for k in range(7):
                heat_out[k, r] = g_new[k]
            mass_out[r] = m_new
            return
        for i in range(19):
            flow[i, r] = f_new[i]
        for k in range(7):
            warm[k, r] = g_new[k]
        mass[r] = m_new
        collide_row(rd + 1, r, f_new, g_new, m_new)

    def first_row(r):
        collide_row(0, r, [flow[i, r] for i in range(19)], [warm[k, r] for k in range(7)], mass[r])

    for load in loads[:6]:
        load.wait()
    first_row(0)
    first_row(ROWS - 1)
    pl.semaphore_wait(barrier, sum(there(dx, dy).astype(jnp.int32) for dx, dy in CLASSES))
    send(0, range(6))
    lax.fori_loop(1, ROWS - 1, lambda r, _: (first_row(r), 0)[1], 0)
    send(0, (6, 7))
    loads[6].wait()
    for rd in range(ITERS):
        receive(rd, (6, 7))
        lax.fori_loop(1, ROWS - 1, lambda r, _: (stream_row(rd, r, False), 0)[1], 0)
        receive(rd, (0, 2, 3))
        stream_row(rd, 0, False)
        if rd < ITERS - 1:
            send(rd + 1, (1, 4, 5))
        receive(rd, (1, 4, 5))
        stream_row(rd, ROWS - 1, True)
        if rd < ITERS - 1:
            send(rd + 1, (0, 2, 3))
            send(rd + 1, (6, 7))
    for cls in range(8):

        @pl.when(there(*CLASSES[cls]))
        def _():
            for rd in range(ITERS):
                copy_of(rd, cls).wait_send()


def write_out(*refs):
    sem = refs[6]
    copies = [pltpu.make_async_copy(refs[i], refs[3 + i], sem.at[i]) for i in range(3)]
    for copy in copies:
        copy.start()
    for copy in copies:
        copy.wait()


def solution(mesh):
    gx_size, gy_size = mesh.shape["gx"], mesh.shape["gy"]
    f32, i32 = jnp.float32, jnp.int32
    row = (ROWS, SUB, LANE)
    shapes = [(19,) + row, (7,) + row, row]
    in_vmem = pl.BlockSpec(memory_space=pltpu.VMEM)
    in_hbm = pl.BlockSpec(memory_space=pltpu.HBM)

    def shards(*args):
        halo = (ITERS, 2, 9, ROWS + 2, SUB, LANE)
        done = pl.pallas_call(
            functools.partial(kernel, gx_size, gy_size),
            out_shape=[pltpu.VMEM(s, f32) for s in shapes],
            in_specs=[in_hbm] * 7,
            out_specs=[in_vmem] * 3,
            scratch_shapes=[
                pltpu.VMEM((19,) + row, f32),
                pltpu.VMEM((7,) + row, f32),
                pltpu.VMEM(row, f32),
                pltpu.VMEM(row, f32),
                pltpu.VMEM(row, f32),
                pltpu.VMEM(row, i32),
                pltpu.VMEM((2,) + row, i32),
                pltpu.VMEM((26,) + row, f32),
                pltpu.VMEM((3,) + row, f32),
                pltpu.VMEM(row, f32),
                pltpu.VMEM((ITERS, 15, ROWS + 2, SUB, LANE), f32),
                pltpu.VMEM(halo, f32),
                pltpu.VMEM(halo, f32),
                pltpu.VMEM((18,) + row, f32),
                pltpu.VMEM((18,) + row, f32),
                pltpu.VMEM((18,) + row, f32),
                pltpu.SemaphoreType.DMA((7,)),
                pltpu.SemaphoreType.DMA((ITERS, 8)),
                pltpu.SemaphoreType.DMA((ITERS, 8)),
            ],
            compiler_params=pltpu.CompilerParams(
                collective_id=0, has_side_effects=True, vmem_limit_bytes=24 * 1024 * 1024
            ),
        )(*args)
        done = [pltpu.with_memory_space_constraint(a, pltpu.VMEM) for a in done]
        return tuple(
            pl.pallas_call(
                write_out,
                out_shape=[jax.ShapeDtypeStruct(s, f32) for s in shapes],
                in_specs=[in_vmem] * 3,
                out_specs=[in_hbm] * 3,
                scratch_shapes=[pltpu.SemaphoreType.DMA((3,))],
            )(*done)
        )

    block, field = P("gx", "gy", None), P(None, "gx", "gy", None)
    return jax.shard_map(
        shards,
        mesh=mesh,
        in_specs=(field, field, block, block, block, block, field),
        out_specs=(field, field, block),
        check_vma=False,
    )
```

```python
import functools

import jax
import jax.numpy as jnp
from jax import lax
from jax.experimental import pallas as pl
from jax.experimental.pallas import tpu as pltpu
from jax.sharding import PartitionSpec as P

ITERS = 3
VELOCITY = [
    (0, 0, 0),
    (1, 0, 0),
    (-1, 0, 0),
    (0, 1, 0),
    (0, -1, 0),
    (0, 0, 1),
    (0, 0, -1),
    (1, 1, 0),
    (-1, -1, 0),
    (1, -1, 0),
    (-1, 1, 0),
    (1, 0, 1),
    (-1, 0, -1),
    (1, 0, -1),
    (-1, 0, 1),
    (0, 1, 1),
    (0, -1, -1),
    (0, 1, -1),
    (0, -1, 1),
]
WEIGHTS = [1.0 / 3.0] + [1.0 / 18.0] * 6 + [1.0 / 36.0] * 12
OPPOSITE = [0, 2, 1, 4, 3, 6, 5, 8, 7, 10, 9, 12, 11, 14, 13, 16, 15, 18, 17]
EXPANSION = 0.05
MESH = pl.DeviceIdType.MESH
ROWS, SUB, LANE = 6, 8, 128

FRAC, KIND_A, KIND_B = 26, 27, 28
X_FIELDS = [
    [KIND_A, 1, 7, 9, 11, 13, 20, FRAC, 2, 8, 10, 12, 14, 21, KIND_B],
    [1, 7, 9, 11, 13, 20, FRAC, 2, 8, 10, 12, 14, 21],
]
Y_FIELDS = [
    {1: [3, 15, 17, 22, KIND_A, 7, FRAC, 10, KIND_B], -1: [4, 16, 18, 23, KIND_A, 9, FRAC, 8, KIND_B]},
    {1: [3, 15, 17, 22, 7, FRAC, 10], -1: [4, 16, 18, 23, 9, FRAC, 8]},
]
NEIGHBOURS = [(1, 0), (-1, 0), (1, 1), (1, -1), (-1, 1), (-1, -1), (0, 1), (0, -1)]
LOW, HIGH, INNER = (1, 1), (ROWS, 1), (2, ROWS - 2)
CLASSES = [way + (None,) for way in NEIGHBOURS[:6]] + [(0, dy, part) for part in (LOW, HIGH, INNER) for dy in (1, -1)]
TO_HIGH, TO_LOW, Y_LOW, Y_HIGH, Y_INNER = (0, 2, 3), (1, 4, 5), (6, 7), (8, 9), (10, 11)


def x_index(rd, field):
    return X_FIELDS[min(rd, 1)].index(field)


def y_index(rd, dy, field):
    return Y_FIELDS[min(rd, 1)][dy].index(field)


def roll_y(value, dy):
    return pltpu.roll(value, dy % SUB, 0) if dy else value


def roll_z(value, dz):
    return pltpu.roll(value, dz % LANE, 1) if dz else value


def collide(f, g, mass, rate, heat, kind):
    (sa, sb, sc, sd, se, sf, sg, sh, si) = [f[i] + f[i + 1] for i in range(1, 19, 2)]
    (da, db, dc, dd, de, df, dg, dh, di) = [f[i] - f[i + 1] for i in range(1, 19, 2)]
    sxy, sxz, syz = sd + se, sf + sg, sh + si
    sbc = sb + sc
    sax = sa + sbc
    sdg = sxy + sxz + syz
    rho = f[0] + sax + sdg
    xde, xfg = dd + de, df + dg
    yde, yhi = dd - de, dh + di
    zfg, zhi = df - dg, dh - di
    xs, ys, zs = xde + xfg, yde + yhi, zfg + zhi
    jx, jy, jz = da + xs, db + ys, dc + zs
    inv = 1.0 / rho
    ux, uy, uz = jx * inv, jy * inv, jz * inv
    xx, yy, zz = jx * ux, jy * uy, jz * uz
    ruu = xx + yy + zz
    ae = (1.19 * 19.0 / 2394.0) * (sdg - f[0] - ruu)
    ap = (1.4 / 252.0) * (9.0 * f[0] - 7.0 * sax - 2.0 * sdg + 5.5 * ruu)
    qxx, qww = 2.0 * xx - yy - zz, yy - zz
    t1, t2 = 2.0 * sa - sbc, sxy + sxz - 2.0 * syz
    w1, w2 = sb - sc, sxy - sxz
    b = (1.25 / 36.0) * (t1 + t2 - qxx)
    bp = (1.4 / 72.0) * (t2 - 2.0 * t1 + 0.5 * qxx)
    c = (1.25 / 12.0) * (w1 + w2 - qww)
    cp = (1.4 / 24.0) * (w2 - 2.0 * w1 + 0.5 * qww)
    dxy = (1.25 / 4.0) * (sd - se - jx * uy)
    dyz = (1.25 / 4.0) * (sh - si - jy * uz)
    dxz = (1.25 / 4.0) * (sf - sg - jx * uz)
    q = 1.2 / 40.0 * 5.0 / 3.0
    qx, qy, qz = q * (xs - 2.0 * da), q * (ys - 2.0 * db), q * (zs - 2.0 * dc)
    m = 1.98 / 8.0
    mx, my, mz = m * (xde - xfg), m * (yhi - yde), m * (zfg - zhi)
    b1, b2 = -11.0 * ae - 4.0 * ap, 8.0 * ae + ap
    bm, cm, bs, cs = b - 2.0 * bp, c - 2.0 * cp, b + bp, c + cp
    b1m = b1 - bm
    exy, exz, eyz = b2 + bs + cs, b2 + bs - cs, b2 - 2.0 * bs
    even = [b1m + 3.0 * bm, b1m + cm, b1m - cm, exy + dxy, exy - dxy, exz + dxz, exz - dxz, eyz + dyz, eyz - dyz]
    warmth = g[0] + (g[1] + g[2]) + (g[3] + g[4]) + (g[5] + g[6])
    push = (EXPANSION / 6.0) * (warmth - 1.0)
    half = 0.5 * push
    xp, xm, yp, ym, zp, zm = qx + mx, qx - mx, qy + my, qy - my, qz + mz - half, qz - mz - half
    odd = [-4.0 * qx, -4.0 * qy, -4.0 * qz - push, xp + ym, xp - ym, xm + zp, xm - zp, yp + zm, yp - zm]
    post = [f[0] + 30.0 * ae - 12.0 * ap]
    for k in range(9):
        post.append(f[2 * k + 1] - (even[k] + odd[k]))
        post.append(f[2 * k + 2] - (even[k] - odd[k]))
    keep = 1.0 - rate
    rest = 0.125 * (rate * warmth + heat)
    half_rate = 0.5 * rate * warmth
    post.append(keep * g[0] + 2.0 * rest)
    for k, u in enumerate((ux, uy, uz)):
        move = half_rate * u
        post.append(keep * g[2 * k + 1] + (rest + move))
        post.append(keep * g[2 * k + 2] + (rest - move))
    frac = jnp.where(kind == 1, mass * inv, jnp.where(kind == 2, 1.0, 0.0))
    return post, frac, (ux, uy, uz)


def kernel(gx_size, gy_size, *refs):
    flow_in, heat_in, mass_in, diff_in, source_in, kind_in, mask_in = refs[:7]
    flow_out, heat_out, mass_out = refs[7:10]
    (flow, warm, mass, rate, source, kinds, masks, post, vel, own_frac, t_buf, y_buf, h_buf, code, liquid, shared,
     load_sem, send_sem, recv_sem) = refs[10:]
    gx, gy = lax.axis_index("gx"), lax.axis_index("gy")

    def there(dx, dy):
        tests = []
        if dx:
            tests.append(gx < gx_size - 1 if dx > 0 else gx > 0)
        if dy:
            tests.append(gy < gy_size - 1 if dy > 0 else gy > 0)
        return functools.reduce(jnp.logical_and, tests)

    barrier = pltpu.get_barrier_semaphore()
    for dx, dy in NEIGHBOURS:

        @pl.when(there(dx, dy))
        def _():
            pl.semaphore_signal(barrier, inc=1, device_id=(gx + dx, gy + dy), device_id_type=MESH)

    count = [0]

    def load(*pairs):
        started = []
        for src, dst in pairs:
            started.append(pltpu.make_async_copy(src, dst, load_sem.at[count[0]]))
            count[0] += 1
        for copy in started:
            copy.start()
        return started

    def rows_of(at, size):
        cut = (slice(None), pl.ds(at, size))
        return (flow_in.at[cut], flow.at[cut]), (heat_in.at[cut], warm.at[cut])

    last_loads = load(
        *rows_of(ROWS - 1, 1), (mass_in, mass), (diff_in, rate), (source_in, source), (kind_in, kinds)
    )
    first_loads = load(*rows_of(0, 1))
    inner_loads = load(*rows_of(1, ROWS - 2), (mask_in, masks))

    def copy_of(rd, cls):
        dx, dy, part = CLASSES[cls]
        first = rd == 0
        if not dy:
            own, far = (ROWS, 0) if dx > 0 else (1, ROWS + 1)
            if dx > 0:
                fields = pl.ds(0, 8 if first else 7)
            else:
                fields = pl.ds(7 if first else 6, 8 if first else 7)
            src, dst = t_buf.at[rd, fields, own], t_buf.at[rd, fields, far]
        else:
            side, edge = (0, 0) if dy > 0 else (1, SUB - 1)
            line = pl.ds(edge, 1)
            if not dx:
                fields = pl.ds(0, 8 if first else 7)
                own = far = pl.ds(*part)
            elif dx > 0:
                fields = pl.ds(4, 3 if first else 2)
                own, far = ROWS, 0
            else:
                fields = pl.ds(6 if first else 5, 3 if first else 2)
                own, far = 1, ROWS + 1
            src, dst = y_buf.at[rd, side, fields, own, line], h_buf.at[rd, side, fields, far, line]
        return pltpu.make_async_remote_copy(
            src_ref=src,
            dst_ref=dst,
            send_sem=send_sem.at[rd, cls],
            recv_sem=recv_sem.at[rd, cls],
            device_id=(gx + dx, gy + dy),
            device_id_type=MESH,
        )

    def send(rd, classes):
        for cls in classes:

            @pl.when(there(*CLASSES[cls][:2]))
            def _():
                copy_of(rd, cls).start()

    def receive(rd, classes):
        for cls in classes:
            dx, dy, _ = CLASSES[cls]

            @pl.when(there(-dx, -dy))
            def _():
                copy_of(rd, cls).wait_recv()

    line_of = lax.broadcasted_iota(jnp.int32, (SUB, LANE), 0)
    edge_of = {1: line_of == 0, -1: line_of == SUB - 1}
    top = lax.broadcasted_iota(jnp.int32, (SUB, LANE), 1) == LANE - 1

    def collide_row(rd, r, f, g, m):
        kind = kinds[r]
        if rd == 0:
            rate[r] = 1.0 / (0.5 + 4.0 * rate[r])
        values, frac, velocity = collide(f, g, m, rate[r], source[r], kind)
        for i in range(26):
            post[i, r] = values[i]
        for i in range(3):
            vel[i, r] = velocity[i]
        own_frac[r] = frac
        fields = dict(enumerate(values))
        fields[FRAC] = frac
        if rd == 0:
            fields[KIND_A] = fields[KIND_B] = kind.astype(jnp.float32)
        moved = {}
        for i, field in enumerate(X_FIELDS[min(rd, 1)]):
            value = fields[field]
            if field < 26:
                dx, dy, dz = VELOCITY[field if field < 19 else field - 19]
                value = moved[field] = roll_y(roll_z(value, dz), dy)
            t_buf[rd, i, r + 1] = value
        for side, way in ((0, 1), (1, -1)):
            for i, field in enumerate(Y_FIELDS[min(rd, 1)][way]):
                if field in moved:
                    value = moved[field]
                else:
                    dz = VELOCITY[field if field < 19 else field - 19][2] if field < 26 else 0
                    value = roll_y(roll_z(fields[field], dz), way)
                y_buf[rd, side, i, r + 1] = value

    def joined(rd, way, field, row, value):
        side, edge = (0, 0) if way > 0 else (1, SUB - 1)
        return jnp.where(edge_of[way], h_buf[rd, side, y_index(rd, way, field), row, edge : edge + 1], value)

    def sources(rd, r, field_of, own):
        plain = {0: own, 1: field_of(r), -1: field_of(r + 2)}
        found = {}
        for dx in (0, 1, -1):
            row = r + 1 - dx
            found[dx, 0] = plain[dx]
            for way in (1, -1):
                if isinstance(field_of.name, dict):
                    name = field_of.name[dx]
                else:
                    name = field_of.name
                found[dx, way] = joined(rd, way, name, row, roll_y(plain[dx], way))
        return {i: roll_z(found[VELOCITY[i][0], VELOCITY[i][1]], VELOCITY[i][2]) for i in range(1, 19)}

    def stream_row(rd, r, last_row):
        kind = kinds[r]
        if rd == 0:

            def kind_at(row):
                return t_buf[rd, x_index(rd, KIND_B if last_row and row is not r else KIND_A), row]

            kind_at.name = {0: KIND_A, 1: KIND_A, -1: KIND_B if last_row else KIND_A}
            kind_from = sources(rd, r, kind_at, kind.astype(jnp.float32))

        def frac_at(row):
            return t_buf[rd, x_index(rd, FRAC), row]

        frac_at.name = FRAC
        frac = own_frac[r]
        frac_from = sources(rd, r, frac_at, frac)
        ux, uy, uz = vel[0, r], vel[1, r], vel[2, r]
        base = 2.0 - 3.0 * (ux * ux + uy * uy + uz * uz)
        old = [post[i, r] for i in range(26)]

        def incoming(i):
            dx, dy, dz = VELOCITY[i if i < 19 else i - 19]
            row = r + 1 - dx
            if dx == 0 and dy == 0:
                return roll_z(old[i], dz)
            if dx and not dy:
                return t_buf[rd, x_index(rd, i), row]
            if dx:
                return joined(rd, dy, i, row, t_buf[rd, x_index(rd, i), row])
            return joined(rd, dy, i, row, y_buf[rd, 0 if dy > 0 else 1, y_index(rd, dy, i), row])

        f_new, g_new = [old[0]], [old[19]]
        change = jnp.zeros((SUB, LANE), jnp.float32)
        closed = {}
        for i in range(1, 19):
            if rd == 0:
                word = masks[(i - 1) // 9, r]
                enabled = ((word >> ((i - 1) % 9)) & 1).astype(jnp.float32)
                here = kind_from[i]
                if VELOCITY[i][2] < 0:
                    here = jnp.where(top, 0.0, here)
                code[i - 1, r] = here
                whole = jnp.where(here == 2.0, enabled, 0.0)
                part = jnp.where(here == 1.0, 0.5 * enabled, 0.0)
                liquid[i - 1, r] = whole
                shared[i - 1, r] = part
            else:
                here, whole, part = code[i - 1, r], liquid[i - 1, r], shared[i - 1, r]
            wall, gas = here == 3.0, here == 0.0
            dx, dy, dz = VELOCITY[i]
            along = sum(s * u for s, u in zip((dx, dy, dz), (ux, uy, uz)) if s)
            rebuilt = WEIGHTS[i] * (base + 9.0 * (along * along))
            arriving, back = incoming(i), old[OPPOSITE[i]]
            f_new.append(jnp.where(wall, back, jnp.where(gas, rebuilt - back, arriving)))
            change = change + (whole + part * (frac + frac_from[i])) * (arriving - back)
            if i < 7:
                closed[i] = jnp.logical_or(wall, gas)
        for k in range(1, 7):
            g_new.append(jnp.where(closed[k], old[19 + OPPOSITE[k]], incoming(19 + k)))
        fluid = jnp.logical_or(kind == 1, kind == 2)
        f_new = [jnp.where(fluid, f_new[i], flow[i, r]) for i in range(19)]
        g_new = [jnp.where(fluid, g_new[k], warm[k, r]) for k in range(7)]
        total = functools.reduce(jnp.add, f_new)
        m_new = jnp.where(kind == 1, mass[r] + change, jnp.where(kind == 2, total, 0.0))
        if rd == ITERS - 1:
            for i in range(19):
                flow_out[i, r] = f_new[i]
            for k in range(7):
                heat_out[k, r] = g_new[k]
            mass_out[r] = m_new
            return
        for i in range(19):
            flow[i, r] = f_new[i]
        for k in range(7):
            warm[k, r] = g_new[k]
        mass[r] = m_new
        collide_row(rd + 1, r, f_new, g_new, m_new)

    def first_row(r):
        collide_row(0, r, [flow[i, r] for i in range(19)], [warm[k, r] for k in range(7)], mass[r])

    def wait(copies):
        for copy in copies:
            copy.wait()

    def rows_in_turn(body, first, step):
        lax.fori_loop(0, 2, lambda k, _: (body(first + step * k), 0)[1], 0)

    wait(last_loads)
    first_row(ROWS - 1)
    wait(first_loads)
    first_row(0)
    pl.semaphore_wait(barrier, sum(there(dx, dy).astype(jnp.int32) for dx, dy in NEIGHBOURS))
    send(0, TO_HIGH + TO_LOW + Y_LOW + Y_HIGH)
    wait(inner_loads)
    lax.fori_loop(1, ROWS - 1, lambda r, _: (first_row(r), 0)[1], 0)
    send(0, Y_INNER)
    for rd in range(ITERS):
        more = rd < ITERS - 1
        receive(rd, Y_INNER)
        rows_in_turn(lambda r: stream_row(rd, r, False), 2, 1)
        ends = [(0, 1, TO_HIGH + Y_LOW, TO_LOW + Y_LOW), (ROWS - 1, ROWS - 2, TO_LOW + Y_HIGH, TO_HIGH + Y_HIGH)]
        for r, beside, needed, leaving in ends if more else reversed(ends):
            receive(rd, needed)
            stream_row(rd, r, r == ROWS - 1)
            if more:
                send(rd + 1, leaving)
            else:
                stream_row(rd, beside, False)
        if more:
            rows_in_turn(lambda r: stream_row(rd, r, False), 1, ROWS - 3)
            send(rd + 1, Y_INNER)
    for cls in range(len(CLASSES)):

        @pl.when(there(*CLASSES[cls][:2]))
        def _():
            for rd in range(ITERS):
                copy_of(rd, cls).wait_send()


def write_out(*refs):
    sem = refs[6]
    copies = [pltpu.make_async_copy(refs[i], refs[3 + i], sem.at[i]) for i in range(3)]
    for copy in copies:
        copy.start()
    for copy in copies:
        copy.wait()


def solution(mesh):
    gx_size, gy_size = mesh.shape["gx"], mesh.shape["gy"]
    f32, i32 = jnp.float32, jnp.int32
    row = (ROWS, SUB, LANE)
    shapes = [(19,) + row, (7,) + row, row]
    in_vmem = pl.BlockSpec(memory_space=pltpu.VMEM)
    in_hbm = pl.BlockSpec(memory_space=pltpu.HBM)

    def shards(*args):
        halo = (ITERS, 2, 9, ROWS + 2, SUB, LANE)
        done = pl.pallas_call(
            functools.partial(kernel, gx_size, gy_size),
            out_shape=[pltpu.VMEM(s, f32) for s in shapes],
            in_specs=[in_hbm] * 7,
            out_specs=[in_vmem] * 3,
            scratch_shapes=[
                pltpu.VMEM((19,) + row, f32),
                pltpu.VMEM((7,) + row, f32),
                pltpu.VMEM(row, f32),
                pltpu.VMEM(row, f32),
                pltpu.VMEM(row, f32),
                pltpu.VMEM(row, i32),
                pltpu.VMEM((2,) + row, i32),
                pltpu.VMEM((26,) + row, f32),
                pltpu.VMEM((3,) + row, f32),
                pltpu.VMEM(row, f32),
                pltpu.VMEM((ITERS, 15, ROWS + 2, SUB, LANE), f32),
                pltpu.VMEM(halo, f32),
                pltpu.VMEM(halo, f32),
                pltpu.VMEM((18,) + row, f32),
                pltpu.VMEM((18,) + row, f32),
                pltpu.VMEM((18,) + row, f32),
                pltpu.SemaphoreType.DMA((11,)),
                pltpu.SemaphoreType.DMA((ITERS, len(CLASSES))),
                pltpu.SemaphoreType.DMA((ITERS, len(CLASSES))),
            ],
            compiler_params=pltpu.CompilerParams(
                collective_id=0, has_side_effects=True, vmem_limit_bytes=24 * 1024 * 1024
            ),
        )(*[pltpu.with_memory_space_constraint(a, pltpu.HBM) for a in args])
        done = [pltpu.with_memory_space_constraint(a, pltpu.VMEM) for a in done]
        return tuple(
            pl.pallas_call(
                write_out,
                out_shape=[jax.ShapeDtypeStruct(s, f32) for s in shapes],
                in_specs=[in_vmem] * 3,
                out_specs=[in_hbm] * 3,
                scratch_shapes=[pltpu.SemaphoreType.DMA((3,))],
            )(*done)
        )

    block, field = P("gx", "gy", None), P(None, "gx", "gy", None)
    return jax.shard_map(
        shards,
        mesh=mesh,
        in_specs=(field, field, block, block, block, block, field),
        out_specs=(field, field, block),
        check_vma=False,
    )
```

```python
import functools

import jax
import jax.numpy as jnp
from jax import lax
from jax.experimental import pallas as pl
from jax.experimental.pallas import tpu as pltpu
from jax.sharding import PartitionSpec as P

ITERS = 3
VELOCITY = [
    (0, 0, 0),
    (1, 0, 0),
    (-1, 0, 0),
    (0, 1, 0),
    (0, -1, 0),
    (0, 0, 1),
    (0, 0, -1),
    (1, 1, 0),
    (-1, -1, 0),
    (1, -1, 0),
    (-1, 1, 0),
    (1, 0, 1),
    (-1, 0, -1),
    (1, 0, -1),
    (-1, 0, 1),
    (0, 1, 1),
    (0, -1, -1),
    (0, 1, -1),
    (0, -1, 1),
]
WEIGHTS = [1.0 / 3.0] + [1.0 / 18.0] * 6 + [1.0 / 36.0] * 12
OPPOSITE = [0, 2, 1, 4, 3, 6, 5, 8, 7, 10, 9, 12, 11, 14, 13, 16, 15, 18, 17]
EXPANSION = 0.05
MESH = pl.DeviceIdType.MESH
ROWS, SUB, LANE = 6, 8, 128

FRAC, KIND_A, KIND_B = 26, 27, 28
MASS, RATE, SOURCE = 26, 27, 28
X_FIELDS = [
    [KIND_A, 1, 7, 9, 11, 13, 20, FRAC, 2, 8, 10, 12, 14, 21, KIND_B],
    [1, 7, 9, 11, 13, 20, FRAC, 2, 8, 10, 12, 14, 21],
]
Y_FIELDS = [
    {1: [3, 15, 17, 22, KIND_A, 7, FRAC, 10, KIND_B], -1: [4, 16, 18, 23, KIND_A, 9, FRAC, 8, KIND_B]},
    {1: [3, 15, 17, 22, 7, FRAC, 10], -1: [4, 16, 18, 23, 9, FRAC, 8]},
]
NEIGHBOURS = [(1, 0), (-1, 0), (1, 1), (1, -1), (-1, 1), (-1, -1), (0, 1), (0, -1)]
LOW, HIGH, INNER = (1, 1), (ROWS, 1), (2, ROWS - 2)
CLASSES = [way + (None,) for way in NEIGHBOURS[:6]] + [(0, dy, part) for part in (LOW, HIGH, INNER) for dy in (1, -1)]
GROUPS = [(0, 2, 3), (1, 4, 5), (6, 7), (8, 9), (10, 11)]
TO_HIGH, TO_LOW, Y_LOW, Y_HIGH, Y_INNER = range(5)


def x_index(rd, field):
    return X_FIELDS[min(rd, 1)].index(field)


def y_index(rd, dy, field):
    return Y_FIELDS[min(rd, 1)][dy].index(field)


def roll_y(value, dy):
    return pltpu.roll(value, dy % SUB, 0) if dy else value


def roll_z(value, dz):
    return pltpu.roll(value, dz % LANE, 1) if dz else value


def tree(terms):
    terms = list(terms)
    while len(terms) > 1:
        terms = [sum(terms[i : i + 2][1:], terms[i]) for i in range(0, len(terms), 2)]
    return terms[0]


def collide(f, g, mass, rate, heat, kind):
    (sa, sb, sc, sd, se, sf, sg, sh, si) = [f[i] + f[i + 1] for i in range(1, 19, 2)]
    (da, db, dc, dd, de, df, dg, dh, di) = [f[i] - f[i + 1] for i in range(1, 19, 2)]
    sxy, sxz, syz = sd + se, sf + sg, sh + si
    sbc = sb + sc
    sax = sa + sbc
    sdg = sxy + sxz + syz
    rho = f[0] + sax + sdg
    xde, xfg = dd + de, df + dg
    yde, yhi = dd - de, dh + di
    zfg, zhi = df - dg, dh - di
    xs, ys, zs = xde + xfg, yde + yhi, zfg + zhi
    jx, jy, jz = da + xs, db + ys, dc + zs
    inv = 1.0 / rho
    ux, uy, uz = jx * inv, jy * inv, jz * inv
    xx, yy, zz = jx * ux, jy * uy, jz * uz
    ruu = xx + yy + zz
    ae = (1.19 * 19.0 / 2394.0) * (sdg - f[0] - ruu)
    ap = (1.4 / 252.0) * (9.0 * f[0] - 7.0 * sax - 2.0 * sdg + 5.5 * ruu)
    qxx, qww = 2.0 * xx - yy - zz, yy - zz
    t1, t2 = 2.0 * sa - sbc, sxy + sxz - 2.0 * syz
    w1, w2 = sb - sc, sxy - sxz
    b = (1.25 / 36.0) * (t1 + t2 - qxx)
    bp = (1.4 / 72.0) * (t2 - 2.0 * t1 + 0.5 * qxx)
    c = (1.25 / 12.0) * (w1 + w2 - qww)
    cp = (1.4 / 24.0) * (w2 - 2.0 * w1 + 0.5 * qww)
    dxy = (1.25 / 4.0) * (sd - se - jx * uy)
    dyz = (1.25 / 4.0) * (sh - si - jy * uz)
    dxz = (1.25 / 4.0) * (sf - sg - jx * uz)
    q = 1.2 / 40.0 * 5.0 / 3.0
    qx, qy, qz = q * (xs - 2.0 * da), q * (ys - 2.0 * db), q * (zs - 2.0 * dc)
    m = 1.98 / 8.0
    mx, my, mz = m * (xde - xfg), m * (yhi - yde), m * (zfg - zhi)
    b1, b2 = -11.0 * ae - 4.0 * ap, 8.0 * ae + ap
    bm, cm, bs, cs = b - 2.0 * bp, c - 2.0 * cp, b + bp, c + cp
    b1m = b1 - bm
    exy, exz, eyz = b2 + bs + cs, b2 + bs - cs, b2 - 2.0 * bs
    even = [b1m + 3.0 * bm, b1m + cm, b1m - cm, exy + dxy, exy - dxy, exz + dxz, exz - dxz, eyz + dyz, eyz - dyz]
    warmth = g[0] + (g[1] + g[2]) + (g[3] + g[4]) + (g[5] + g[6])
    push = (EXPANSION / 6.0) * (warmth - 1.0)
    half = 0.5 * push
    xp, xm, yp, ym, zp, zm = qx + mx, qx - mx, qy + my, qy - my, qz + mz - half, qz - mz - half
    odd = [-4.0 * qx, -4.0 * qy, -4.0 * qz - push, xp + ym, xp - ym, xm + zp, xm - zp, yp + zm, yp - zm]
    post = [f[0] + 30.0 * ae - 12.0 * ap]
    for k in range(9):
        post.append(f[2 * k + 1] - (even[k] + odd[k]))
        post.append(f[2 * k + 2] - (even[k] - odd[k]))
    keep = 1.0 - rate
    rest = 0.125 * (rate * warmth + heat)
    half_rate = 0.5 * rate * warmth
    post.append(keep * g[0] + 2.0 * rest)
    for k, u in enumerate((ux, uy, uz)):
        move = half_rate * u
        post.append(keep * g[2 * k + 1] + (rest + move))
        post.append(keep * g[2 * k + 2] + (rest - move))
    frac = jnp.where(kind == 1, mass * inv, jnp.where(kind == 2, 1.0, 0.0))
    return post, frac, (ux, uy, uz)


def kernel(gx_size, gy_size, *refs):
    flow_in, heat_in, mass_in, diff_in, source_in, kind_in, mask_in = refs[:7]
    flow_out, heat_out, mass_out = refs[7:10]
    (state, kinds, masks, post, vel, own_frac, t_buf, y_buf, h_buf, code, liquid, shared, t_size,
     load_sem, send_sem, recv_sem) = refs[10:]
    gx, gy = lax.axis_index("gx"), lax.axis_index("gy")

    def there(dx, dy):
        tests = []
        if dx:
            tests.append(gx < gx_size - 1 if dx > 0 else gx > 0)
        if dy:
            tests.append(gy < gy_size - 1 if dy > 0 else gy > 0)
        return functools.reduce(jnp.logical_and, tests)

    barrier = pltpu.get_barrier_semaphore()
    for dx, dy in NEIGHBOURS:

        @pl.when(there(dx, dy))
        def _():
            pl.semaphore_signal(barrier, inc=1, device_id=(gx + dx, gy + dy), device_id_type=MESH)

    def rows_of(at, size, sem):
        rows = pl.ds(at, size)
        return [
            pltpu.make_async_copy(flow_in.at[:, rows], state.at[pl.ds(0, 19), rows], load_sem.at[sem]),
            pltpu.make_async_copy(heat_in.at[:, rows], state.at[pl.ds(19, 7), rows], load_sem.at[sem]),
        ]

    def wait_rows(at, size, sem):
        there = state.at[pl.ds(0, 26), pl.ds(at, size)]
        pltpu.make_async_copy(there, there, load_sem.at[sem]).wait()

    load_kinds = pltpu.make_async_copy(kind_in, kinds, load_sem.at[3])
    load_masks = pltpu.make_async_copy(mask_in, masks, load_sem.at[4])
    load_cells = [
        pltpu.make_async_copy(src, state.at[at], load_sem.at[5])
        for src, at in ((mass_in, MASS), (diff_in, RATE), (source_in, SOURCE))
    ]
    for load in rows_of(ROWS - 1, 1, 0) + load_cells + [load_kinds] + rows_of(0, 1, 1) + rows_of(1, ROWS - 2, 2):
        load.start()
    load_masks.start()

    def copy_of(rd, cls):
        dx, dy, part = CLASSES[cls]
        group = [cls in members for members in GROUPS].index(True)
        first = rd == 0
        if not dy:
            own, far = (ROWS, 0) if dx > 0 else (1, ROWS + 1)
            if dx > 0:
                fields = pl.ds(0, 8 if first else 7)
            else:
                fields = pl.ds(7 if first else 6, 8 if first else 7)
            src, dst = t_buf.at[rd, fields, own], t_buf.at[rd, fields, far]
        else:
            side, edge = (0, 0) if dy > 0 else (1, SUB - 1)
            line = pl.ds(edge, 1)
            if not dx:
                fields = pl.ds(0, 8 if first else 7)
                own = far = pl.ds(*part)
            elif dx > 0:
                fields = pl.ds(4, 3 if first else 2)
                own, far = ROWS, 0
            else:
                fields = pl.ds(6 if first else 5, 3 if first else 2)
                own, far = 1, ROWS + 1
            src, dst = y_buf.at[rd, side, fields, own, line], h_buf.at[rd, side, fields, far, line]
        return pltpu.make_async_remote_copy(
            src_ref=src,
            dst_ref=dst,
            send_sem=send_sem.at[rd % 2, group],
            recv_sem=recv_sem.at[rd % 2, group],
            device_id=(gx + dx, gy + dy),
            device_id_type=MESH,
        )

    def send(rd, *groups):
        for group in groups:
            for cls in GROUPS[group]:

                @pl.when(there(*CLASSES[cls][:2]))
                def _():
                    copy_of(rd, cls).start()

    def wait_group(rd, group, sem, there_x):
        fields = 8 if rd == 0 else 7
        fixed, each = (fields * SUB, fields - 5) if group < 2 else (0, fields * CLASSES[GROUPS[group][0]][2][1])
        inside = jnp.logical_and(gy > 0, gy < gy_size - 1)
        for both in (True, False):
            test = inside if both else jnp.logical_not(inside)

            @pl.when(jnp.logical_and(test, there_x) if group < 2 else test)
            def _():
                lines = t_size.at[pl.ds(0, fixed + each * (2 if both else 1))]
                pltpu.make_async_copy(lines, lines, sem).wait()

    def drain(rd):
        for group in range(len(GROUPS)):
            wait_group(rd, group, send_sem.at[rd % 2, group], there(CLASSES[GROUPS[group][0]][0], 0) if group < 2 else None)

    def receive(rd, *groups):
        for group in groups:
            wait_group(
                rd, group, recv_sem.at[rd % 2, group], there(-CLASSES[GROUPS[group][0]][0], 0) if group < 2 else None
            )

    line_of = lax.broadcasted_iota(jnp.int32, (SUB, LANE), 0)
    edge_of = {1: line_of == 0, -1: line_of == SUB - 1}
    top = lax.broadcasted_iota(jnp.int32, (SUB, LANE), 1) == LANE - 1

    def collide_row(rd, r, f, g, m):
        kind = kinds[r]
        if rd == 0:
            state[RATE, r] = 1.0 / (0.5 + 4.0 * state[RATE, r])
        values, frac, velocity = collide(f, g, m, state[RATE, r], state[SOURCE, r], kind)
        for i in range(26):
            post[i, r] = values[i]
        for i in range(3):
            vel[i, r] = velocity[i]
        own_frac[r] = frac
        fields = dict(enumerate(values))
        fields[FRAC] = frac
        if rd == 0:
            fields[KIND_A] = fields[KIND_B] = kind.astype(jnp.float32)
        moved = {}
        for i, field in enumerate(X_FIELDS[min(rd, 1)]):
            value = fields[field]
            if field < 26:
                dx, dy, dz = VELOCITY[field if field < 19 else field - 19]
                value = moved[field] = roll_y(roll_z(value, dz), dy)
            t_buf[rd, i, r + 1] = value
        for side, way in ((0, 1), (1, -1)):
            for i, field in enumerate(Y_FIELDS[min(rd, 1)][way]):
                if field in moved:
                    value = moved[field]
                else:
                    dz = VELOCITY[field if field < 19 else field - 19][2] if field < 26 else 0
                    value = roll_y(roll_z(fields[field], dz), way)
                y_buf[rd, side, i, r + 1] = value

    def joined(rd, way, field, row, value):
        side, edge = (0, 0) if way > 0 else (1, SUB - 1)
        return jnp.where(edge_of[way], h_buf[rd, side, y_index(rd, way, field), row, edge : edge + 1], value)

    def stream_row(rd, r, stages):
        kind = kinds[r]
        frac = own_frac[r]
        ux, uy, uz = vel[0, r], vel[1, r], vel[2, r]
        base = 2.0 - 3.0 * (ux * ux + uy * uy + uz * uz)
        fluid = jnp.logical_or(kind == 1, kind == 2)
        old = [post[i, r] for i in range(26)]
        known = {}

        def at_source(i, field, own):
            dx, dy, dz = VELOCITY[i]
            if (field, dx, dy) not in known:
                row = r + 1 - dx
                name = field
                if field == KIND_A and dx == -1 and isinstance(r, int) and r == ROWS - 1:
                    name = KIND_B
                value = t_buf[rd, x_index(rd, name), row] if dx else own
                known[field, dx, dy] = joined(rd, dy, name, row, roll_y(value, dy)) if dy else value
            return roll_z(known[field, dx, dy], dz)

        def incoming(i):
            dx, dy, dz = VELOCITY[i if i < 19 else i - 19]
            row = r + 1 - dx
            if dx == 0 and dy == 0:
                return roll_z(old[i], dz)
            if dx and not dy:
                return t_buf[rd, x_index(rd, i), row]
            if dx:
                return joined(rd, dy, i, row, t_buf[rd, x_index(rd, i), row])
            return joined(rd, dy, i, row, y_buf[rd, 0 if dy > 0 else 1, y_index(rd, dy, i), row])

        f_new, g_new, changes = {0: old[0]}, {0: old[19]}, []
        for directions in stages:
            yield
            terms = []
            for i in directions:
                if rd == 0:
                    word = masks[(i - 1) // 9, r]
                    enabled = ((word >> ((i - 1) % 9)) & 1).astype(jnp.float32)
                    here = at_source(i, KIND_A, kind.astype(jnp.float32))
                    if VELOCITY[i][2] < 0:
                        here = jnp.where(top, 0.0, here)
                    code[i - 1, r] = here
                    whole = jnp.where(here == 2.0, enabled, 0.0)
                    part = jnp.where(here == 1.0, 0.5 * enabled, 0.0)
                    liquid[i - 1, r] = whole
                    shared[i - 1, r] = part
                else:
                    here, whole, part = code[i - 1, r], liquid[i - 1, r], shared[i - 1, r]
                wall, gas = here == 3.0, here == 0.0
                along = sum(s * u for s, u in zip(VELOCITY[i], (ux, uy, uz)) if s)
                rebuilt = WEIGHTS[i] * (base + 9.0 * (along * along))
                arriving, back = incoming(i), old[OPPOSITE[i]]
                f_new[i] = jnp.where(wall, back, jnp.where(gas, rebuilt - back, arriving))
                terms.append((whole + part * (frac + at_source(i, FRAC, frac))) * (arriving - back))
                if i < 7:
                    g_new[i] = jnp.where(jnp.logical_or(wall, gas), old[19 + OPPOSITE[i]], incoming(19 + i))
            changes.append(tree(terms))
        f_new = [jnp.where(fluid, f_new[i], state[i, r]) for i in range(19)]
        g_new = [jnp.where(fluid, g_new[k], state[19 + k, r]) for k in range(7)]
        m_new = jnp.where(kind == 1, state[MASS, r] + tree(changes), jnp.where(kind == 2, tree(f_new), 0.0))
        if rd == ITERS - 1:
            for i in range(19):
                flow_out[i, r] = f_new[i]
            for k in range(7):
                heat_out[k, r] = g_new[k]
            mass_out[r] = m_new
            return
        for i, value in enumerate(f_new + g_new + [m_new]):
            state[i, r] = value
        collide_row(rd + 1, r, f_new, g_new, m_new)

    def first_row(r):
        collide_row(0, r, [state[i, r] for i in range(19)], [state[19 + k, r] for k in range(7)], state[MASS, r])

    def whole_rows(rd, first, step):
        def body(k, _):
            for _ in stream_row(rd, first + step * k, [range(1, 19)]):
                pass
            return 0

        lax.fori_loop(0, 2, body, 0)

    def end_row(rd, r, way):
        return stream_row(
            rd,
            r,
            [
                [i for i in range(1, 19) if VELOCITY[i][0] != way and VELOCITY[i][1] == 0],
                [i for i in range(1, 19) if VELOCITY[i][0] != way and VELOCITY[i][1]],
                [i for i in range(1, 19) if VELOCITY[i][0] == way],
            ],
        )

    def beside_row(rd, r, way):
        late = [i for i in range(7, 11) if VELOCITY[i][0] == way]
        return stream_row(rd, r, [[i for i in range(1, 19) if i not in late], late])

    def step_on(*rows):
        for row in rows:
            next(row, None)

    wait_rows(ROWS - 1, 1, 0)
    cells = state.at[pl.ds(MASS, 3)]
    pltpu.make_async_copy(cells, cells, load_sem.at[5]).wait()
    load_kinds.wait()
    first_row(ROWS - 1)
    wait_rows(0, 1, 1)
    first_row(0)
    def first_inner():
        wait_rows(1, ROWS - 2, 2)
        lax.fori_loop(1, ROWS - 1, lambda r, _: (first_row(r), 0)[1], 0)

    early = gx % (gx_size // 2) == 0
    later = jnp.logical_not(early)
    pl.when(early)(first_inner)
    pl.semaphore_wait(barrier, sum(there(dx, dy).astype(jnp.int32) for dx, dy in NEIGHBOURS))

    @pl.when(early)
    def _():
        send(0, TO_LOW, Y_LOW, Y_INNER, Y_HIGH, TO_HIGH)

    @pl.when(later)
    def _():
        send(0, TO_HIGH, TO_LOW, Y_HIGH, Y_LOW)
        first_inner()
        send(0, Y_INNER)

    load_masks.wait()
    for rd in range(ITERS):
        inner_pair = functools.partial(whole_rows, rd, 2, 1)

        def outer_pair():
            whole_rows(rd, 1, ROWS - 3)
            send(rd + 1, Y_INNER)

        def end(r, way, across, leaving, wait_along):
            row = end_row(rd, r, way)
            step_on(row, row)
            wait_along()
            step_on(row)
            receive(rd, across)
            step_on(row)
            send(rd + 1, *leaving)

        if rd == 0:

            @pl.when(later)
            def _():
                receive(rd, Y_INNER)
                inner_pair()
                receive(rd, Y_LOW, Y_HIGH)
                outer_pair()

            end(
                0, 1, TO_HIGH, (TO_LOW, Y_LOW), lambda: pl.when(early)(lambda: receive(rd, Y_INNER, Y_LOW, Y_HIGH))
            )

            @pl.when(early)
            def _():
                inner_pair()
                outer_pair()

            end(ROWS - 1, -1, TO_LOW, (Y_HIGH, TO_HIGH), lambda: None)
        elif rd < ITERS - 1:
            receive(rd, Y_INNER)
            inner_pair()
            drain(rd - 1)

            @pl.when(early)
            def _():
                receive(rd, Y_LOW, Y_HIGH)
                outer_pair()

            end(0, 1, TO_HIGH, (Y_LOW, TO_LOW), lambda: pl.when(later)(lambda: receive(rd, Y_LOW)))
            end(ROWS - 1, -1, TO_LOW, (TO_HIGH, Y_HIGH), lambda: pl.when(later)(lambda: receive(rd, Y_HIGH)))
            pl.when(later)(outer_pair)
        else:
            receive(rd, Y_INNER)
            inner_pair()
            drain(rd - 1)
            drain(rd)
            for r, way, across, along in ((ROWS - 1, -1, TO_LOW, Y_HIGH), (0, 1, TO_HIGH, Y_LOW)):
                row, beside = end_row(rd, r, way), beside_row(rd, r + way, way)
                step_on(row, row, beside, beside)
                receive(rd, along)
                step_on(beside, row)
                receive(rd, across)
                step_on(row)


def write_out(*refs):
    sem = refs[6]
    copies = [pltpu.make_async_copy(refs[i], refs[3 + i], sem.at[i]) for i in range(3)]
    for copy in copies:
        copy.start()
    for copy in copies:
        copy.wait()


def solution(mesh):
    gx_size, gy_size = mesh.shape["gx"], mesh.shape["gy"]
    f32, i32 = jnp.float32, jnp.int32
    row = (ROWS, SUB, LANE)
    shapes = [(19,) + row, (7,) + row, row]
    in_vmem = pl.BlockSpec(memory_space=pltpu.VMEM)
    in_hbm = pl.BlockSpec(memory_space=pltpu.HBM)

    def shards(*args):
        halo = (ITERS, 2, 9, ROWS + 2, SUB, LANE)
        done = pl.pallas_call(
            functools.partial(kernel, gx_size, gy_size),
            out_shape=[pltpu.VMEM(s, f32) for s in shapes],
            in_specs=[in_hbm] * 7,
            out_specs=[in_vmem] * 3,
            scratch_shapes=[
                pltpu.VMEM((29,) + row, f32),
                pltpu.VMEM(row, i32),
                pltpu.VMEM((2,) + row, i32),
                pltpu.VMEM((26,) + row, f32),
                pltpu.VMEM((3,) + row, f32),
                pltpu.VMEM(row, f32),
                pltpu.VMEM((ITERS, 15, ROWS + 2, SUB, LANE), f32),
                pltpu.VMEM(halo, f32),
                pltpu.VMEM(halo, f32),
                pltpu.VMEM((18,) + row, f32),
                pltpu.VMEM((18,) + row, f32),
                pltpu.VMEM((18,) + row, f32),
                pltpu.VMEM((72, LANE), f32),
                pltpu.SemaphoreType.DMA((6,)),
                pltpu.SemaphoreType.DMA((2, len(GROUPS))),
                pltpu.SemaphoreType.DMA((2, len(GROUPS))),
            ],
            compiler_params=pltpu.CompilerParams(
                collective_id=0, has_side_effects=True, vmem_limit_bytes=24 * 1024 * 1024
            ),
        )(*[pltpu.with_memory_space_constraint(a, pltpu.HBM) for a in args])
        done = [pltpu.with_memory_space_constraint(a, pltpu.VMEM) for a in done]
        return tuple(
            pl.pallas_call(
                write_out,
                out_shape=[jax.ShapeDtypeStruct(s, f32) for s in shapes],
                in_specs=[in_vmem] * 3,
                out_specs=[in_hbm] * 3,
                scratch_shapes=[pltpu.SemaphoreType.DMA((3,))],
            )(*done)
        )

    block, field = P("gx", "gy", None), P(None, "gx", "gy", None)
    return jax.shard_map(
        shards,
        mesh=mesh,
        in_specs=(field, field, block, block, block, block, field),
        out_specs=(field, field, block),
        check_vma=False,
    )
```

```python
import functools

import jax
import jax.numpy as jnp
from jax import lax
from jax.experimental import pallas as pl
from jax.experimental.pallas import tpu as pltpu
from jax.sharding import PartitionSpec as P

ITERS = 3
VELOCITY = [
    (0, 0, 0),
    (1, 0, 0),
    (-1, 0, 0),
    (0, 1, 0),
    (0, -1, 0),
    (0, 0, 1),
    (0, 0, -1),
    (1, 1, 0),
    (-1, -1, 0),
    (1, -1, 0),
    (-1, 1, 0),
    (1, 0, 1),
    (-1, 0, -1),
    (1, 0, -1),
    (-1, 0, 1),
    (0, 1, 1),
    (0, -1, -1),
    (0, 1, -1),
    (0, -1, 1),
]
WEIGHTS = [1.0 / 3.0] + [1.0 / 18.0] * 6 + [1.0 / 36.0] * 12
OPPOSITE = [0, 2, 1, 4, 3, 6, 5, 8, 7, 10, 9, 12, 11, 14, 13, 16, 15, 18, 17]
EXPANSION = 0.05
MESH = pl.DeviceIdType.MESH
ROWS, SUB, LANE = 6, 8, 128

FRAC, KIND_A, KIND_B = 26, 27, 28
MASS, RATE, SOURCE = 26, 27, 28
X_FIELDS = [
    [KIND_A, 1, 7, 9, 11, 13, 20, FRAC, 2, 8, 10, 12, 14, 21, KIND_B],
    [1, 7, 9, 11, 13, 20, FRAC, 2, 8, 10, 12, 14, 21],
]
Y_FIELDS = [
    {1: [3, 15, 17, 22, KIND_A, 7, FRAC, 10, KIND_B], -1: [4, 16, 18, 23, KIND_A, 9, FRAC, 8, KIND_B]},
    {1: [3, 15, 17, 22, 7, FRAC, 10], -1: [4, 16, 18, 23, 9, FRAC, 8]},
]
NEIGHBOURS = [(1, 0), (-1, 0), (1, 1), (1, -1), (-1, 1), (-1, -1), (0, 1), (0, -1)]
LOW, HIGH, INNER = (1, 1), (ROWS, 1), (2, ROWS - 2)
CLASSES = [way + (None,) for way in NEIGHBOURS[:6]] + [(0, dy, part) for part in (LOW, HIGH, INNER) for dy in (1, -1)]
GROUPS = [(0, 2, 3), (1, 4, 5), (6, 7), (8, 9), (10, 11)]
TO_HIGH, TO_LOW, Y_LOW, Y_HIGH, Y_INNER = range(5)


def x_index(rd, field):
    return X_FIELDS[min(rd, 1)].index(field)


def y_index(rd, dy, field):
    return Y_FIELDS[min(rd, 1)][dy].index(field)


def roll_y(value, dy):
    return pltpu.roll(value, dy % SUB, 0) if dy else value


def roll_z(value, dz):
    return pltpu.roll(value, dz % LANE, 1) if dz else value


def tree(terms):
    terms = list(terms)
    while len(terms) > 1:
        terms = [sum(terms[i : i + 2][1:], terms[i]) for i in range(0, len(terms), 2)]
    return terms[0]


def collide(f, g, mass, rate, heat, kind):
    (sa, sb, sc, sd, se, sf, sg, sh, si) = [f[i] + f[i + 1] for i in range(1, 19, 2)]
    (da, db, dc, dd, de, df, dg, dh, di) = [f[i] - f[i + 1] for i in range(1, 19, 2)]
    sxy, sxz, syz = sd + se, sf + sg, sh + si
    sbc = sb + sc
    sax = sa + sbc
    sdg = sxy + sxz + syz
    rho = f[0] + sax + sdg
    xde, xfg = dd + de, df + dg
    yde, yhi = dd - de, dh + di
    zfg, zhi = df - dg, dh - di
    xs, ys, zs = xde + xfg, yde + yhi, zfg + zhi
    jx, jy, jz = da + xs, db + ys, dc + zs
    inv = 1.0 / rho
    ux, uy, uz = jx * inv, jy * inv, jz * inv
    xx, yy, zz = jx * ux, jy * uy, jz * uz
    ruu = xx + yy + zz
    ae = (1.19 * 19.0 / 2394.0) * (sdg - f[0] - ruu)
    ap = (1.4 / 252.0) * (9.0 * f[0] - 7.0 * sax - 2.0 * sdg + 5.5 * ruu)
    qxx, qww = 2.0 * xx - yy - zz, yy - zz
    t1, t2 = 2.0 * sa - sbc, sxy + sxz - 2.0 * syz
    w1, w2 = sb - sc, sxy - sxz
    b = (1.25 / 36.0) * (t1 + t2 - qxx)
    bp = (1.4 / 72.0) * (t2 - 2.0 * t1 + 0.5 * qxx)
    c = (1.25 / 12.0) * (w1 + w2 - qww)
    cp = (1.4 / 24.0) * (w2 - 2.0 * w1 + 0.5 * qww)
    dxy = (1.25 / 4.0) * (sd - se - jx * uy)
    dyz = (1.25 / 4.0) * (sh - si - jy * uz)
    dxz = (1.25 / 4.0) * (sf - sg - jx * uz)
    q = 1.2 / 40.0 * 5.0 / 3.0
    qx, qy, qz = q * (xs - 2.0 * da), q * (ys - 2.0 * db), q * (zs - 2.0 * dc)
    m = 1.98 / 8.0
    mx, my, mz = m * (xde - xfg), m * (yhi - yde), m * (zfg - zhi)
    b1, b2 = -11.0 * ae - 4.0 * ap, 8.0 * ae + ap
    bm, cm, bs, cs = b - 2.0 * bp, c - 2.0 * cp, b + bp, c + cp
    b1m = b1 - bm
    exy, exz, eyz = b2 + bs + cs, b2 + bs - cs, b2 - 2.0 * bs
    even = [b1m + 3.0 * bm, b1m + cm, b1m - cm, exy + dxy, exy - dxy, exz + dxz, exz - dxz, eyz + dyz, eyz - dyz]
    warmth = g[0] + (g[1] + g[2]) + (g[3] + g[4]) + (g[5] + g[6])
    push = (EXPANSION / 6.0) * (warmth - 1.0)
    half = 0.5 * push
    xp, xm, yp, ym, zp, zm = qx + mx, qx - mx, qy + my, qy - my, qz + mz - half, qz - mz - half
    odd = [-4.0 * qx, -4.0 * qy, -4.0 * qz - push, xp + ym, xp - ym, xm + zp, xm - zp, yp + zm, yp - zm]
    post = [f[0] + 30.0 * ae - 12.0 * ap]
    for k in range(9):
        post.append(f[2 * k + 1] - (even[k] + odd[k]))
        post.append(f[2 * k + 2] - (even[k] - odd[k]))
    keep = 1.0 - rate
    rest = 0.125 * (rate * warmth + heat)
    half_rate = 0.5 * rate * warmth
    post.append(keep * g[0] + 2.0 * rest)
    for k, u in enumerate((ux, uy, uz)):
        move = half_rate * u
        post.append(keep * g[2 * k + 1] + (rest + move))
        post.append(keep * g[2 * k + 2] + (rest - move))
    frac = jnp.where(kind == 1, mass * inv, jnp.where(kind == 2, 1.0, 0.0))
    return post, frac, (ux, uy, uz)


def kernel(gx_size, gy_size, *refs):
    flow_in, heat_in, mass_in, diff_in, source_in, kind_in, mask_in = refs[:7]
    flow_out, heat_out, mass_out = refs[7:10]
    (state, kinds, masks, post, vel, own_frac, t_buf, y_buf, h_buf, code, liquid, shared, t_size,
     load_sem, send_sem, recv_sem) = refs[10:]
    gx, gy = lax.axis_index("gx"), lax.axis_index("gy")

    def there(dx, dy):
        tests = []
        if dx:
            tests.append(gx < gx_size - 1 if dx > 0 else gx > 0)
        if dy:
            tests.append(gy < gy_size - 1 if dy > 0 else gy > 0)
        return functools.reduce(jnp.logical_and, tests)

    barrier = pltpu.get_barrier_semaphore()

    def greet(ways):
        for dx, dy in ways:

            @pl.when(there(dx, dy))
            def _():
                pl.semaphore_signal(barrier, inc=1, device_id=(gx + dx, gy + dy), device_id_type=MESH)

    greet([way for way in NEIGHBOURS if way[0] > 0])

    def rows_of(at, size, sem):
        rows = pl.ds(at, size)
        return [
            pltpu.make_async_copy(flow_in.at[:, rows], state.at[pl.ds(0, 19), rows], load_sem.at[sem]),
            pltpu.make_async_copy(heat_in.at[:, rows], state.at[pl.ds(19, 7), rows], load_sem.at[sem]),
        ]

    def wait_rows(at, size, sem):
        there = state.at[pl.ds(0, 26), pl.ds(at, size)]
        pltpu.make_async_copy(there, there, load_sem.at[sem]).wait()

    load_kinds = pltpu.make_async_copy(kind_in, kinds, load_sem.at[3])
    load_masks = pltpu.make_async_copy(mask_in, masks, load_sem.at[3])
    load_cells = [
        pltpu.make_async_copy(src, state.at[at], load_sem.at[0])
        for src, at in ((mass_in, MASS), (diff_in, RATE), (source_in, SOURCE))
    ]
    for load in rows_of(ROWS - 1, 1, 0) + load_cells + [load_kinds]:
        load.start()
    greet([way for way in NEIGHBOURS if way[0] <= 0])
    for load in rows_of(0, 1, 1) + rows_of(1, ROWS - 2, 2):
        load.start()

    def copy_of(rd, cls):
        dx, dy, part = CLASSES[cls]
        group = [cls in members for members in GROUPS].index(True)
        first = rd == 0
        if not dy:
            own, far = (ROWS, 0) if dx > 0 else (1, ROWS + 1)
            if dx > 0:
                fields = pl.ds(0, 8 if first else 7)
            else:
                fields = pl.ds(7 if first else 6, 8 if first else 7)
            src, dst = t_buf.at[rd, fields, own], t_buf.at[rd, fields, far]
        else:
            side, edge = (0, 0) if dy > 0 else (1, SUB - 1)
            line = pl.ds(edge, 1)
            if not dx:
                fields = pl.ds(0, 8 if first else 7)
                own = far = pl.ds(*part)
            elif dx > 0:
                fields = pl.ds(4, 3 if first else 2)
                own, far = ROWS, 0
            else:
                fields = pl.ds(6 if first else 5, 3 if first else 2)
                own, far = 1, ROWS + 1
            src, dst = y_buf.at[rd, side, fields, own, line], h_buf.at[rd, side, fields, far, line]
        return pltpu.make_async_remote_copy(
            src_ref=src,
            dst_ref=dst,
            send_sem=send_sem.at[rd % 2],
            recv_sem=recv_sem.at[rd % 2, group],
            device_id=(gx + dx, gy + dy),
            device_id_type=MESH,
        )

    def send(rd, *groups):
        for group in groups:
            for cls in GROUPS[group]:

                @pl.when(there(*CLASSES[cls][:2]))
                def _():
                    copy_of(rd, cls).start()

    def wait_lines(test, count, sem):
        @pl.when(test)
        def _():
            lines = t_size.at[pl.ds(0, count)]
            pltpu.make_async_copy(lines, lines, sem).wait()

    inside_x = jnp.logical_and(gx > 0, gx < gx_size - 1)
    inside_y = jnp.logical_and(gy > 0, gy < gy_size - 1)

    def wait_group(rd, group, sem, there_x):
        fields = 8 if rd == 0 else 7
        fixed, each = (fields * SUB, fields - 5) if group < 2 else (0, fields * CLASSES[GROUPS[group][0]][2][1])
        for sides, test in ((2, inside_y), (1, jnp.logical_not(inside_y))):
            wait_lines(jnp.logical_and(test, there_x) if group < 2 else test, fixed + each * sides, sem)

    def drain(rd):
        fields = 8 if rd == 0 else 7
        for sides_x, test_x in ((2, inside_x), (1, jnp.logical_not(inside_x))):
            for sides_y, test_y in ((2, inside_y), (1, jnp.logical_not(inside_y))):
                count = sides_x * (fields * SUB + sides_y * (fields - 5)) + sides_y * fields * ROWS
                wait_lines(jnp.logical_and(test_x, test_y), count, send_sem.at[rd % 2])

    def receive(rd, *groups):
        for group in groups:
            wait_group(
                rd, group, recv_sem.at[rd % 2, group], there(-CLASSES[GROUPS[group][0]][0], 0) if group < 2 else None
            )

    line_of = lax.broadcasted_iota(jnp.int32, (SUB, LANE), 0)
    edge_of = {1: line_of == 0, -1: line_of == SUB - 1}
    top = lax.broadcasted_iota(jnp.int32, (SUB, LANE), 1) == LANE - 1

    def collide_row(rd, r, f, g, m):
        kind = kinds[r]
        if rd == 0:
            state[RATE, r] = 1.0 / (0.5 + 4.0 * state[RATE, r])
        values, frac, velocity = collide(f, g, m, state[RATE, r], state[SOURCE, r], kind)
        for i in range(26):
            post[i, r] = values[i]
        for i in range(3):
            vel[i, r] = velocity[i]
        own_frac[r] = frac
        fields = dict(enumerate(values))
        fields[FRAC] = frac
        if rd == 0:
            fields[KIND_A] = fields[KIND_B] = kind.astype(jnp.float32)
        moved = {}
        for i, field in enumerate(X_FIELDS[min(rd, 1)]):
            value = fields[field]
            if field < 26:
                dx, dy, dz = VELOCITY[field if field < 19 else field - 19]
                value = moved[field] = roll_y(roll_z(value, dz), dy)
            t_buf[rd, i, r + 1] = value
        for side, way in ((0, 1), (1, -1)):
            for i, field in enumerate(Y_FIELDS[min(rd, 1)][way]):
                if field in moved:
                    value = moved[field]
                else:
                    dz = VELOCITY[field if field < 19 else field - 19][2] if field < 26 else 0
                    value = roll_y(roll_z(fields[field], dz), way)
                y_buf[rd, side, i, r + 1] = value

    def joined(rd, way, field, row, value):
        side, edge = (0, 0) if way > 0 else (1, SUB - 1)
        return jnp.where(edge_of[way], h_buf[rd, side, y_index(rd, way, field), row, edge : edge + 1], value)

    def stream_row(rd, r, stages):
        kind = kinds[r]
        frac = own_frac[r]
        ux, uy, uz = vel[0, r], vel[1, r], vel[2, r]
        base = 2.0 - 3.0 * (ux * ux + uy * uy + uz * uz)
        fluid = jnp.logical_or(kind == 1, kind == 2)
        old = [post[i, r] for i in range(26)]
        known = {}

        def at_source(i, field, own):
            dx, dy, dz = VELOCITY[i]
            if (field, dx, dy) not in known:
                row = r + 1 - dx
                name = field
                if field == KIND_A and dx == -1 and isinstance(r, int) and r == ROWS - 1:
                    name = KIND_B
                value = t_buf[rd, x_index(rd, name), row] if dx else own
                known[field, dx, dy] = joined(rd, dy, name, row, roll_y(value, dy)) if dy else value
            return roll_z(known[field, dx, dy], dz)

        def incoming(i):
            dx, dy, dz = VELOCITY[i if i < 19 else i - 19]
            row = r + 1 - dx
            if dx == 0 and dy == 0:
                return roll_z(old[i], dz)
            if dx and not dy:
                return t_buf[rd, x_index(rd, i), row]
            if dx:
                return joined(rd, dy, i, row, t_buf[rd, x_index(rd, i), row])
            return joined(rd, dy, i, row, y_buf[rd, 0 if dy > 0 else 1, y_index(rd, dy, i), row])

        f_new, g_new, changes = {0: old[0]}, {0: old[19]}, []
        for directions in stages:
            yield
            terms = []
            for i in directions:
                if rd == 0:
                    word = masks[(i - 1) // 9, r]
                    enabled = ((word >> ((i - 1) % 9)) & 1).astype(jnp.float32)
                    here = at_source(i, KIND_A, kind.astype(jnp.float32))
                    if VELOCITY[i][2] < 0:
                        here = jnp.where(top, 0.0, here)
                    code[i - 1, r] = here
                    whole = jnp.where(here == 2.0, enabled, 0.0)
                    part = jnp.where(here == 1.0, 0.5 * enabled, 0.0)
                    liquid[i - 1, r] = whole
                    shared[i - 1, r] = part
                else:
                    here, whole, part = code[i - 1, r], liquid[i - 1, r], shared[i - 1, r]
                wall, gas = here == 3.0, here == 0.0
                along = sum(s * u for s, u in zip(VELOCITY[i], (ux, uy, uz)) if s)
                rebuilt = WEIGHTS[i] * (base + 9.0 * (along * along))
                arriving, back = incoming(i), old[OPPOSITE[i]]
                f_new[i] = jnp.where(wall, back, jnp.where(gas, rebuilt - back, arriving))
                terms.append((whole + part * (frac + at_source(i, FRAC, frac))) * (arriving - back))
                if i < 7:
                    g_new[i] = jnp.where(jnp.logical_or(wall, gas), old[19 + OPPOSITE[i]], incoming(19 + i))
            changes.append(tree(terms))
        f_new = [jnp.where(fluid, f_new[i], state[i, r]) for i in range(19)]
        g_new = [jnp.where(fluid, g_new[k], state[19 + k, r]) for k in range(7)]
        m_new = jnp.where(kind == 1, state[MASS, r] + tree(changes), jnp.where(kind == 2, tree(f_new), 0.0))
        if rd == ITERS - 1:
            for i in range(19):
                flow_out[i, r] = f_new[i]
            for k in range(7):
                heat_out[k, r] = g_new[k]
            mass_out[r] = m_new
            return
        for i, value in enumerate(f_new + g_new + [m_new]):
            state[i, r] = value
        collide_row(rd + 1, r, f_new, g_new, m_new)

    def first_row(r):
        collide_row(0, r, [state[i, r] for i in range(19)], [state[19 + k, r] for k in range(7)], state[MASS, r])

    def whole_rows(rd, first, step):
        def body(k, _):
            for _ in stream_row(rd, first + step * k, [range(1, 19)]):
                pass
            return 0

        lax.fori_loop(0, 2, body, 0)

    def end_row(rd, r, way, inner_there=True):
        here = [i for i in range(1, 19) if VELOCITY[i][0] != way and VELOCITY[i][1] == 0]
        if inner_there:
            here += [i for i in range(7, 11) if VELOCITY[i][0] == -way]
        return stream_row(
            rd,
            r,
            [
                here,
                [i for i in range(1, 19) if VELOCITY[i][0] != way and i not in here],
                [i for i in range(1, 19) if VELOCITY[i][0] == way],
            ],
        )

    def beside_row(rd, r, way):
        late = [i for i in range(7, 11) if VELOCITY[i][0] == way]
        return stream_row(rd, r, [[i for i in range(1, 19) if i not in late], late])

    def step_on(*rows):
        for row in rows:
            next(row, None)

    lines = t_size.at[pl.ds(0, 26 * SUB + 3 * ROWS * SUB)]
    pltpu.make_async_copy(lines, lines, load_sem.at[0]).wait()
    load_kinds.wait()
    load_masks.start()
    first_row(ROWS - 1)

    def first_low():
        wait_rows(0, 1, 1)
        first_row(0)

    def first_inner():
        wait_rows(1, ROWS - 2, 2)
        lax.fori_loop(1, ROWS - 1, lambda r, _: (first_row(r), 0)[1], 0)

    early = gx % (gx_size // 2) == 0
    later = jnp.logical_not(early)

    @pl.when(early)
    def _():
        first_low()
        first_inner()

    pl.semaphore_wait(barrier, sum(there(dx, dy).astype(jnp.int32) for dx, dy in NEIGHBOURS))

    @pl.when(early)
    def _():
        send(0, TO_LOW, Y_LOW, Y_INNER, Y_HIGH, TO_HIGH)

    @pl.when(later)
    def _():
        send(0, TO_HIGH, Y_HIGH)
        first_low()
        send(0, TO_LOW, Y_LOW)
        first_inner()
        send(0, Y_INNER)

    load_masks.wait()
    for rd in range(ITERS):
        inner_pair = functools.partial(whole_rows, rd, 2, 1)

        def outer_pair():
            whole_rows(rd, 1, ROWS - 3)
            send(rd + 1, Y_INNER)

        def end(r, way, across, leaving, wait_along):
            row = end_row(rd, r, way, rd > 0 or r > 0)
            step_on(row, row)
            wait_along()
            step_on(row)
            receive(rd, across)
            step_on(row)
            send(rd + 1, *leaving)

        if rd == 0:

            @pl.when(later)
            def _():
                receive(rd, Y_INNER)
                inner_pair()
                receive(rd, Y_LOW, Y_HIGH)
                outer_pair()

            end(
                0, 1, TO_HIGH, (TO_LOW, Y_LOW), lambda: pl.when(early)(lambda: receive(rd, Y_INNER, Y_LOW))
            )

            @pl.when(early)
            def _():
                inner_pair()
                receive(rd, Y_HIGH)
                outer_pair()

            end(ROWS - 1, -1, TO_LOW, (Y_HIGH, TO_HIGH), lambda: None)
        elif rd < ITERS - 1:
            receive(rd, Y_INNER)
            inner_pair()
            drain(rd - 1)

            @pl.when(early)
            def _():
                receive(rd, Y_LOW, Y_HIGH)
                outer_pair()

            end(0, 1, TO_HIGH, (Y_LOW, TO_LOW), lambda: pl.when(later)(lambda: receive(rd, Y_LOW)))
            end(ROWS - 1, -1, TO_LOW, (TO_HIGH, Y_HIGH), lambda: pl.when(later)(lambda: receive(rd, Y_HIGH)))
            pl.when(later)(outer_pair)
        else:
            receive(rd, Y_INNER)
            inner_pair()
            drain(rd - 1)
            drain(rd)
            for r, way, across, along in ((ROWS - 1, -1, TO_LOW, Y_HIGH), (0, 1, TO_HIGH, Y_LOW)):
                row, beside = end_row(rd, r, way), beside_row(rd, r + way, way)
                step_on(row, row, beside, beside)
                receive(rd, along)
                step_on(beside, row)
                receive(rd, across)
                step_on(row)


def write_out(*refs):
    sem = refs[6]
    copies = [pltpu.make_async_copy(refs[i], refs[3 + i], sem.at[i]) for i in range(3)]
    for copy in copies:
        copy.start()
    for copy in copies:
        copy.wait()


def solution(mesh):
    gx_size, gy_size = mesh.shape["gx"], mesh.shape["gy"]
    f32, i32 = jnp.float32, jnp.int32
    row = (ROWS, SUB, LANE)
    shapes = [(19,) + row, (7,) + row, row]
    in_vmem = pl.BlockSpec(memory_space=pltpu.VMEM)
    in_hbm = pl.BlockSpec(memory_space=pltpu.HBM)

    def shards(*args):
        halo = (ITERS, 2, 9, ROWS + 2, SUB, LANE)
        done = pl.pallas_call(
            functools.partial(kernel, gx_size, gy_size),
            out_shape=[pltpu.VMEM(s, f32) for s in shapes],
            in_specs=[in_hbm] * 7,
            out_specs=[in_vmem] * 3,
            scratch_shapes=[
                pltpu.VMEM((29,) + row, f32),
                pltpu.VMEM(row, i32),
                pltpu.VMEM((2,) + row, i32),
                pltpu.VMEM((26,) + row, f32),
                pltpu.VMEM((3,) + row, f32),
                pltpu.VMEM(row, f32),
                pltpu.VMEM((ITERS, 15, ROWS + 2, SUB, LANE), f32),
                pltpu.VMEM(halo, f32),
                pltpu.VMEM(halo, f32),
                pltpu.VMEM((18,) + row, f32),
                pltpu.VMEM((18,) + row, f32),
                pltpu.VMEM((18,) + row, f32),
                pltpu.VMEM((352, LANE), f32),
                pltpu.SemaphoreType.DMA((4,)),
                pltpu.SemaphoreType.DMA((2,)),
                pltpu.SemaphoreType.DMA((2, len(GROUPS))),
            ],
            compiler_params=pltpu.CompilerParams(
                collective_id=0, has_side_effects=True, vmem_limit_bytes=24 * 1024 * 1024
            ),
        )(*[pltpu.with_memory_space_constraint(a, pltpu.HBM) for a in args])
        done = [pltpu.with_memory_space_constraint(a, pltpu.VMEM) for a in done]
        return tuple(
            pl.pallas_call(
                write_out,
                out_shape=[jax.ShapeDtypeStruct(s, f32) for s in shapes],
                in_specs=[in_vmem] * 3,
                out_specs=[in_hbm] * 3,
                scratch_shapes=[pltpu.SemaphoreType.DMA((3,))],
            )(*done)
        )

    block, field = P("gx", "gy", None), P(None, "gx", "gy", None)
    return jax.shard_map(
        shards,
        mesh=mesh,
        in_specs=(field, field, block, block, block, block, field),
        out_specs=(field, field, block),
        check_vma=False,
    )
```

```python
import functools

import jax
import jax.numpy as jnp
from jax import lax
from jax.experimental import pallas as pl
from jax.experimental.pallas import tpu as pltpu
from jax.sharding import PartitionSpec as P

ITERS = 3
VELOCITY = [
    (0, 0, 0),
    (1, 0, 0),
    (-1, 0, 0),
    (0, 1, 0),
    (0, -1, 0),
    (0, 0, 1),
    (0, 0, -1),
    (1, 1, 0),
    (-1, -1, 0),
    (1, -1, 0),
    (-1, 1, 0),
    (1, 0, 1),
    (-1, 0, -1),
    (1, 0, -1),
    (-1, 0, 1),
    (0, 1, 1),
    (0, -1, -1),
    (0, 1, -1),
    (0, -1, 1),
]
WEIGHTS = [1.0 / 3.0] + [1.0 / 18.0] * 6 + [1.0 / 36.0] * 12
OPPOSITE = [0, 2, 1, 4, 3, 6, 5, 8, 7, 10, 9, 12, 11, 14, 13, 16, 15, 18, 17]
EXPANSION = 0.05
MESH = pl.DeviceIdType.MESH
ROWS, SUB, LANE = 6, 8, 128

FRAC, KIND_A, KIND_B = 26, 27, 28
MASS, RATE, SOURCE = 26, 27, 28
X_FIELDS = [
    [KIND_A, 1, 7, 9, 11, 13, 20, FRAC, 2, 8, 10, 12, 14, 21, KIND_B],
    [1, 7, 9, 11, 13, 20, FRAC, 2, 8, 10, 12, 14, 21],
]
Y_FIELDS = [
    {1: [3, 15, 17, 22, KIND_A, 7, FRAC, 10, KIND_B], -1: [4, 16, 18, 23, KIND_A, 9, FRAC, 8, KIND_B]},
    {1: [3, 15, 17, 22, 7, FRAC, 10], -1: [4, 16, 18, 23, 9, FRAC, 8]},
]
NEIGHBOURS = [(1, 0), (-1, 0), (1, 1), (1, -1), (-1, 1), (-1, -1), (0, 1), (0, -1)]
LOW, HIGH, INNER = (1, 1), (ROWS, 1), (2, ROWS - 2)
CLASSES = [way + (None,) for way in NEIGHBOURS[:6]] + [(0, dy, part) for part in (LOW, HIGH, INNER) for dy in (-1, 1)]
GROUPS = [(0, 2, 3), (1, 4, 5), (6, 7), (8, 9), (10, 11)]
TO_HIGH, TO_LOW, Y_LOW, Y_HIGH, Y_INNER = range(5)


def x_index(rd, field):
    return X_FIELDS[min(rd, 1)].index(field)


def y_index(rd, dy, field):
    return Y_FIELDS[min(rd, 1)][dy].index(field)


def roll_y(value, dy):
    return pltpu.roll(value, dy % SUB, 0) if dy else value


def roll_z(value, dz):
    return pltpu.roll(value, dz % LANE, 1) if dz else value


def tree(terms):
    terms = list(terms)
    while len(terms) > 1:
        terms = [sum(terms[i : i + 2][1:], terms[i]) for i in range(0, len(terms), 2)]
    return terms[0]


def collide(f, g, mass, rate, heat, kind):
    (sa, sb, sc, sd, se, sf, sg, sh, si) = [f[i] + f[i + 1] for i in range(1, 19, 2)]
    (da, db, dc, dd, de, df, dg, dh, di) = [f[i] - f[i + 1] for i in range(1, 19, 2)]
    sxy, sxz, syz = sd + se, sf + sg, sh + si
    sbc = sb + sc
    sax = sa + sbc
    sdg = sxy + sxz + syz
    rho = f[0] + sax + sdg
    xde, xfg = dd + de, df + dg
    yde, yhi = dd - de, dh + di
    zfg, zhi = df - dg, dh - di
    xs, ys, zs = xde + xfg, yde + yhi, zfg + zhi
    jx, jy, jz = da + xs, db + ys, dc + zs
    inv = 1.0 / rho
    ux, uy, uz = jx * inv, jy * inv, jz * inv
    xx, yy, zz = jx * ux, jy * uy, jz * uz
    ruu = xx + yy + zz
    ae = (1.19 * 19.0 / 2394.0) * (sdg - f[0] - ruu)
    ap = (1.4 / 252.0) * (9.0 * f[0] - 7.0 * sax - 2.0 * sdg + 5.5 * ruu)
    qxx, qww = 2.0 * xx - yy - zz, yy - zz
    t1, t2 = 2.0 * sa - sbc, sxy + sxz - 2.0 * syz
    w1, w2 = sb - sc, sxy - sxz
    b = (1.25 / 36.0) * (t1 + t2 - qxx)
    bp = (1.4 / 72.0) * (t2 - 2.0 * t1 + 0.5 * qxx)
    c = (1.25 / 12.0) * (w1 + w2 - qww)
    cp = (1.4 / 24.0) * (w2 - 2.0 * w1 + 0.5 * qww)
    dxy = (1.25 / 4.0) * (sd - se - jx * uy)
    dyz = (1.25 / 4.0) * (sh - si - jy * uz)
    dxz = (1.25 / 4.0) * (sf - sg - jx * uz)
    q = 1.2 / 40.0 * 5.0 / 3.0
    qx, qy, qz = q * (xs - 2.0 * da), q * (ys - 2.0 * db), q * (zs - 2.0 * dc)
    m = 1.98 / 8.0
    mx, my, mz = m * (xde - xfg), m * (yhi - yde), m * (zfg - zhi)
    b1, b2 = -11.0 * ae - 4.0 * ap, 8.0 * ae + ap
    bm, cm, bs, cs = b - 2.0 * bp, c - 2.0 * cp, b + bp, c + cp
    b1m = b1 - bm
    exy, exz, eyz = b2 + bs + cs, b2 + bs - cs, b2 - 2.0 * bs
    even = [b1m + 3.0 * bm, b1m + cm, b1m - cm, exy + dxy, exy - dxy, exz + dxz, exz - dxz, eyz + dyz, eyz - dyz]
    warmth = g[0] + (g[1] + g[2]) + (g[3] + g[4]) + (g[5] + g[6])
    push = (EXPANSION / 6.0) * (warmth - 1.0)
    half = 0.5 * push
    xp, xm, yp, ym, zp, zm = qx + mx, qx - mx, qy + my, qy - my, qz + mz - half, qz - mz - half
    odd = [-4.0 * qx, -4.0 * qy, -4.0 * qz - push, xp + ym, xp - ym, xm + zp, xm - zp, yp + zm, yp - zm]
    post = [f[0] + 30.0 * ae - 12.0 * ap]
    for k in range(9):
        post.append(f[2 * k + 1] - (even[k] + odd[k]))
        post.append(f[2 * k + 2] - (even[k] - odd[k]))
    keep = 1.0 - rate
    rest = 0.125 * (rate * warmth + heat)
    half_rate = 0.5 * rate * warmth
    post.append(keep * g[0] + 2.0 * rest)
    for k, u in enumerate((ux, uy, uz)):
        move = half_rate * u
        post.append(keep * g[2 * k + 1] + (rest + move))
        post.append(keep * g[2 * k + 2] + (rest - move))
    frac = jnp.where(kind == 1, mass * inv, jnp.where(kind == 2, 1.0, 0.0))
    return post, frac, (ux, uy, uz)


def kernel(gx_size, gy_size, *refs):
    flow_in, heat_in, mass_in, diff_in, source_in, kind_in, mask_in = refs[:7]
    flow_out, heat_out, mass_out = refs[7:10]
    (state, kinds, masks, post, vel, own_frac, t_buf, y_buf, h_buf, code, liquid, shared, t_size,
     load_sem, send_sem, recv_sem) = refs[10:]
    gx, gy = lax.axis_index("gx"), lax.axis_index("gy")

    def there(dx, dy):
        tests = []
        if dx:
            tests.append(gx < gx_size - 1 if dx > 0 else gx > 0)
        if dy:
            tests.append(gy < gy_size - 1 if dy > 0 else gy > 0)
        return functools.reduce(jnp.logical_and, tests)

    barrier = pltpu.get_barrier_semaphore()

    def greet(ways):
        for dx, dy in ways:

            @pl.when(there(dx, dy))
            def _():
                pl.semaphore_signal(barrier, inc=1, device_id=(gx + dx, gy + dy), device_id_type=MESH)

    greet([way for way in NEIGHBOURS if way[0] > 0])

    def rows_of(at, size, sem):
        rows = pl.ds(at, size)
        return [
            pltpu.make_async_copy(flow_in.at[:, rows], state.at[pl.ds(0, 19), rows], load_sem.at[sem]),
            pltpu.make_async_copy(heat_in.at[:, rows], state.at[pl.ds(19, 7), rows], load_sem.at[sem]),
        ]

    def wait_rows(at, size, sem):
        there = state.at[pl.ds(0, 26), pl.ds(at, size)]
        pltpu.make_async_copy(there, there, load_sem.at[sem]).wait()

    load_kinds = pltpu.make_async_copy(kind_in, kinds, load_sem.at[3])
    load_masks = pltpu.make_async_copy(mask_in, masks, load_sem.at[3])
    load_cells = [
        pltpu.make_async_copy(src, state.at[at], load_sem.at[0])
        for src, at in ((mass_in, MASS), (diff_in, RATE), (source_in, SOURCE))
    ]
    for load in rows_of(ROWS - 1, 1, 0) + load_cells + [load_kinds]:
        load.start()
    greet([way for way in NEIGHBOURS if way[0] <= 0])
    for load in rows_of(0, 1, 1) + rows_of(1, ROWS - 2, 2):
        load.start()

    def copy_of(rd, cls):
        dx, dy, part = CLASSES[cls]
        group = [cls in members for members in GROUPS].index(True)
        first = rd == 0
        if not dy:
            own, far = (ROWS, 0) if dx > 0 else (1, ROWS + 1)
            if dx > 0:
                fields = pl.ds(0, 8 if first else 7)
            else:
                fields = pl.ds(7 if first else 6, 8 if first else 7)
            src, dst = t_buf.at[rd, fields, own], t_buf.at[rd, fields, far]
        else:
            side, edge = (0, 0) if dy > 0 else (1, SUB - 1)
            line = pl.ds(edge, 1)
            if not dx:
                fields = pl.ds(0, 8 if first else 7)
                own = far = pl.ds(*part)
            elif dx > 0:
                fields = pl.ds(4, 3 if first else 2)
                own, far = ROWS, 0
            else:
                fields = pl.ds(6 if first else 5, 3 if first else 2)
                own, far = 1, ROWS + 1
            src, dst = y_buf.at[rd, side, fields, own, line], h_buf.at[rd, side, fields, far, line]
        return pltpu.make_async_remote_copy(
            src_ref=src,
            dst_ref=dst,
            send_sem=send_sem.at[rd % 2],
            recv_sem=recv_sem.at[rd % 2, group],
            device_id=(gx + dx, gy + dy),
            device_id_type=MESH,
        )

    def send(rd, *groups):
        for group in groups:
            for cls in GROUPS[group]:

                @pl.when(there(*CLASSES[cls][:2]))
                def _():
                    copy_of(rd, cls).start()

    def wait_lines(test, count, sem):
        @pl.when(test)
        def _():
            lines = t_size.at[pl.ds(0, count)]
            pltpu.make_async_copy(lines, lines, sem).wait()

    inside_x = jnp.logical_and(gx > 0, gx < gx_size - 1)
    inside_y = jnp.logical_and(gy > 0, gy < gy_size - 1)

    def wait_group(rd, group, sem, there_x):
        fields = 8 if rd == 0 else 7
        fixed, each = (fields * SUB, fields - 5) if group < 2 else (0, fields * CLASSES[GROUPS[group][0]][2][1])
        for sides, test in ((2, inside_y), (1, jnp.logical_not(inside_y))):
            wait_lines(jnp.logical_and(test, there_x) if group < 2 else test, fixed + each * sides, sem)

    def drain(rd):
        fields = 8 if rd == 0 else 7
        for sides_x, test_x in ((2, inside_x), (1, jnp.logical_not(inside_x))):
            for sides_y, test_y in ((2, inside_y), (1, jnp.logical_not(inside_y))):
                count = sides_x * (fields * SUB + sides_y * (fields - 5)) + sides_y * fields * ROWS
                wait_lines(jnp.logical_and(test_x, test_y), count, send_sem.at[rd % 2])

    def receive(rd, *groups):
        for group in groups:
            wait_group(
                rd, group, recv_sem.at[rd % 2, group], there(-CLASSES[GROUPS[group][0]][0], 0) if group < 2 else None
            )

    line_of = lax.broadcasted_iota(jnp.int32, (SUB, LANE), 0)
    edge_of = {1: line_of == 0, -1: line_of == SUB - 1}
    top = lax.broadcasted_iota(jnp.int32, (SUB, LANE), 1) == LANE - 1

    def collide_row(rd, r, f, g, m):
        kind = kinds[r]
        if rd == 0:
            state[RATE, r] = 1.0 / (0.5 + 4.0 * state[RATE, r])
        values, frac, velocity = collide(f, g, m, state[RATE, r], state[SOURCE, r], kind)
        for i in range(26):
            post[i, r] = values[i]
        for i in range(3):
            vel[i, r] = velocity[i]
        own_frac[r] = frac
        fields = dict(enumerate(values))
        fields[FRAC] = frac
        if rd == 0:
            fields[KIND_A] = fields[KIND_B] = kind.astype(jnp.float32)
        moved = {}
        for i, field in enumerate(X_FIELDS[min(rd, 1)]):
            value = fields[field]
            if field < 26:
                dx, dy, dz = VELOCITY[field if field < 19 else field - 19]
                value = moved[field] = roll_y(roll_z(value, dz), dy)
            t_buf[rd, i, r + 1] = value
        for side, way in ((0, 1), (1, -1)):
            for i, field in enumerate(Y_FIELDS[min(rd, 1)][way]):
                if field in moved:
                    value = moved[field]
                else:
                    dz = VELOCITY[field if field < 19 else field - 19][2] if field < 26 else 0
                    value = roll_y(roll_z(fields[field], dz), way)
                y_buf[rd, side, i, r + 1] = value

    def joined(rd, way, field, row, value):
        side, edge = (0, 0) if way > 0 else (1, SUB - 1)
        return jnp.where(edge_of[way], h_buf[rd, side, y_index(rd, way, field), row, edge : edge + 1], value)

    def stream_row(rd, r, stages):
        kind = kinds[r]
        frac = own_frac[r]
        ux, uy, uz = vel[0, r], vel[1, r], vel[2, r]
        base = 2.0 - 3.0 * (ux * ux + uy * uy + uz * uz)
        fluid = jnp.logical_or(kind == 1, kind == 2)
        old = [post[i, r] for i in range(26)]
        known = {}

        def at_source(i, field, own):
            dx, dy, dz = VELOCITY[i]
            if (field, dx, dy) not in known:
                row = r + 1 - dx
                name = field
                if field == KIND_A and dx == -1 and isinstance(r, int) and r == ROWS - 1:
                    name = KIND_B
                value = t_buf[rd, x_index(rd, name), row] if dx else own
                known[field, dx, dy] = joined(rd, dy, name, row, roll_y(value, dy)) if dy else value
            return roll_z(known[field, dx, dy], dz)

        def incoming(i):
            dx, dy, dz = VELOCITY[i if i < 19 else i - 19]
            row = r + 1 - dx
            if dx == 0 and dy == 0:
                return roll_z(old[i], dz)
            if dx and not dy:
                return t_buf[rd, x_index(rd, i), row]
            if dx:
                return joined(rd, dy, i, row, t_buf[rd, x_index(rd, i), row])
            return joined(rd, dy, i, row, y_buf[rd, 0 if dy > 0 else 1, y_index(rd, dy, i), row])

        f_new, g_new, changes = {0: old[0]}, {0: old[19]}, []
        for directions in stages:
            yield
            terms = []
            for i in directions:
                if rd == 0:
                    word = masks[(i - 1) // 9, r]
                    enabled = ((word >> ((i - 1) % 9)) & 1).astype(jnp.float32)
                    here = at_source(i, KIND_A, kind.astype(jnp.float32))
                    if VELOCITY[i][2] < 0:
                        here = jnp.where(top, 0.0, here)
                    code[i - 1, r] = here
                    whole = jnp.where(here == 2.0, enabled, 0.0)
                    part = jnp.where(here == 1.0, 0.5 * enabled, 0.0)
                    liquid[i - 1, r] = whole
                    shared[i - 1, r] = part
                else:
                    here, whole, part = code[i - 1, r], liquid[i - 1, r], shared[i - 1, r]
                wall, gas = here == 3.0, here == 0.0
                along = sum(s * u for s, u in zip(VELOCITY[i], (ux, uy, uz)) if s)
                rebuilt = WEIGHTS[i] * (base + 9.0 * (along * along))
                arriving, back = incoming(i), old[OPPOSITE[i]]
                f_new[i] = jnp.where(wall, back, jnp.where(gas, rebuilt - back, arriving))
                terms.append((whole + part * (frac + at_source(i, FRAC, frac))) * (arriving - back))
                if i < 7:
                    g_new[i] = jnp.where(jnp.logical_or(wall, gas), old[19 + OPPOSITE[i]], incoming(19 + i))
            changes.append(tree(terms))
        f_new = [jnp.where(fluid, f_new[i], state[i, r]) for i in range(19)]
        g_new = [jnp.where(fluid, g_new[k], state[19 + k, r]) for k in range(7)]
        m_new = jnp.where(kind == 1, state[MASS, r] + tree(changes), jnp.where(kind == 2, tree(f_new), 0.0))
        if rd == ITERS - 1:
            for i in range(19):
                flow_out[i, r] = f_new[i]
            for k in range(7):
                heat_out[k, r] = g_new[k]
            mass_out[r] = m_new
            return
        for i, value in enumerate(f_new + g_new + [m_new]):
            state[i, r] = value
        collide_row(rd + 1, r, f_new, g_new, m_new)

    def first_row(r):
        collide_row(0, r, [state[i, r] for i in range(19)], [state[19 + k, r] for k in range(7)], state[MASS, r])

    def whole_rows(rd, first, step):
        def body(k, _):
            for _ in stream_row(rd, first + step * k, [range(1, 19)]):
                pass
            return 0

        lax.fori_loop(0, 2, body, 0)

    def end_row(rd, r, way, inner_there=True):
        here = [i for i in range(1, 19) if VELOCITY[i][0] != way and VELOCITY[i][1] == 0]
        if inner_there:
            here += [i for i in range(7, 11) if VELOCITY[i][0] == -way]
        return stream_row(
            rd,
            r,
            [
                here,
                [i for i in range(1, 19) if VELOCITY[i][0] != way and i not in here],
                [i for i in range(1, 19) if VELOCITY[i][0] == way],
            ],
        )

    def beside_row(rd, r, way):
        late = [i for i in range(7, 11) if VELOCITY[i][0] == way]
        return stream_row(rd, r, [[i for i in range(1, 19) if i not in late], late])

    def step_on(*rows):
        for row in rows:
            next(row, None)

    lines = t_size.at[pl.ds(0, 26 * SUB + 3 * ROWS * SUB)]
    pltpu.make_async_copy(lines, lines, load_sem.at[0]).wait()
    load_kinds.wait()
    load_masks.start()
    first_row(ROWS - 1)

    def first_low():
        wait_rows(0, 1, 1)
        first_row(0)

    def first_inner():
        wait_rows(1, ROWS - 2, 2)
        lax.fori_loop(1, ROWS - 1, lambda r, _: (first_row(r), 0)[1], 0)

    early = gx % (gx_size // 2) == 0
    later = jnp.logical_not(early)

    @pl.when(early)
    def _():
        first_low()
        first_inner()

    pl.semaphore_wait(barrier, sum(there(dx, dy).astype(jnp.int32) for dx, dy in NEIGHBOURS))

    @pl.when(early)
    def _():
        send(0, TO_LOW, Y_LOW, Y_INNER, Y_HIGH, TO_HIGH)

    @pl.when(later)
    def _():
        send(0, TO_HIGH, Y_HIGH)
        first_low()
        send(0, TO_LOW, Y_LOW)
        first_inner()
        send(0, Y_INNER)

    load_masks.wait()
    for rd in range(ITERS):
        inner_pair = functools.partial(whole_rows, rd, 2, 1)

        def outer_pair():
            whole_rows(rd, 1, ROWS - 3)
            send(rd + 1, Y_INNER)

        def end(r, way, across, leaving, wait_along):
            row = end_row(rd, r, way, rd > 0 or r > 0)
            step_on(row, row)
            wait_along()
            step_on(row)
            receive(rd, across)
            step_on(row)
            send(rd + 1, *leaving)

        if rd == 0:

            @pl.when(later)
            def _():
                receive(rd, Y_INNER)
                inner_pair()
                receive(rd, Y_LOW, Y_HIGH)
                outer_pair()

            end(
                0, 1, TO_HIGH, (TO_LOW, Y_LOW), lambda: pl.when(early)(lambda: receive(rd, Y_INNER, Y_LOW))
            )

            @pl.when(early)
            def _():
                inner_pair()
                receive(rd, Y_HIGH)
                outer_pair()

            end(ROWS - 1, -1, TO_LOW, (TO_HIGH, Y_HIGH), lambda: None)
        elif rd < ITERS - 1:
            receive(rd, Y_INNER)
            inner_pair()
            drain(rd - 1)

            @pl.when(early)
            def _():
                receive(rd, Y_LOW, Y_HIGH)
                outer_pair()
                end(ROWS - 1, -1, TO_LOW, (Y_HIGH, TO_HIGH), lambda: None)

            end(0, 1, TO_HIGH, (Y_LOW, TO_LOW), lambda: pl.when(later)(lambda: receive(rd, Y_LOW)))

            @pl.when(later)
            def _():
                end(ROWS - 1, -1, TO_LOW, (TO_HIGH, Y_HIGH), lambda: receive(rd, Y_HIGH))
                outer_pair()
        else:
            receive(rd, Y_INNER)
            inner_pair()
            drain(rd - 1)
            drain(rd)
            for r, way, across, along in ((ROWS - 1, -1, TO_LOW, Y_HIGH), (0, 1, TO_HIGH, Y_LOW)):
                row, beside = end_row(rd, r, way), beside_row(rd, r + way, way)
                step_on(row, row, beside, beside)
                receive(rd, along)
                step_on(beside, row)
                receive(rd, across)
                step_on(row)


def write_out(*refs):
    sem = refs[6]
    copies = [pltpu.make_async_copy(refs[i], refs[3 + i], sem.at[i]) for i in range(3)]
    for copy in copies:
        copy.start()
    for copy in copies:
        copy.wait()


def solution(mesh):
    gx_size, gy_size = mesh.shape["gx"], mesh.shape["gy"]
    f32, i32 = jnp.float32, jnp.int32
    row = (ROWS, SUB, LANE)
    shapes = [(19,) + row, (7,) + row, row]
    in_vmem = pl.BlockSpec(memory_space=pltpu.VMEM)
    in_hbm = pl.BlockSpec(memory_space=pltpu.HBM)

    def shards(*args):
        halo = (ITERS, 2, 9, ROWS + 2, SUB, LANE)
        done = pl.pallas_call(
            functools.partial(kernel, gx_size, gy_size),
            out_shape=[pltpu.VMEM(s, f32) for s in shapes],
            in_specs=[in_hbm] * 7,
            out_specs=[in_vmem] * 3,
            scratch_shapes=[
                pltpu.VMEM((29,) + row, f32),
                pltpu.VMEM(row, i32),
                pltpu.VMEM((2,) + row, i32),
                pltpu.VMEM((26,) + row, f32),
                pltpu.VMEM((3,) + row, f32),
                pltpu.VMEM(row, f32),
                pltpu.VMEM((ITERS, 15, ROWS + 2, SUB, LANE), f32),
                pltpu.VMEM(halo, f32),
                pltpu.VMEM(halo, f32),
                pltpu.VMEM((18,) + row, f32),
                pltpu.VMEM((18,) + row, f32),
                pltpu.VMEM((18,) + row, f32),
                pltpu.VMEM((352, LANE), f32),
                pltpu.SemaphoreType.DMA((4,)),
                pltpu.SemaphoreType.DMA((2,)),
                pltpu.SemaphoreType.DMA((2, len(GROUPS))),
            ],
            compiler_params=pltpu.CompilerParams(
                collective_id=0, has_side_effects=True, vmem_limit_bytes=24 * 1024 * 1024
            ),
        )(*[pltpu.with_memory_space_constraint(a, pltpu.HBM) for a in args])
        done = [pltpu.with_memory_space_constraint(a, pltpu.VMEM) for a in done]
        return tuple(
            pl.pallas_call(
                write_out,
                out_shape=[jax.ShapeDtypeStruct(s, f32) for s in shapes],
                in_specs=[in_vmem] * 3,
                out_specs=[in_hbm] * 3,
                scratch_shapes=[pltpu.SemaphoreType.DMA((3,))],
            )(*done)
        )

    block, field = P("gx", "gy", None), P(None, "gx", "gy", None)
    return jax.shard_map(
        shards,
        mesh=mesh,
        in_specs=(field, field, block, block, block, block, field),
        out_specs=(field, field, block),
        check_vma=False,
    )
```
